128 devices in a mesh: grp: 4 (over y), blk: 32 (over x, z, core).
Axes of the slice: x: 4, y: 4, z: 4, core: 2. Of those that a mesh axis runs over, the one named last changes fastest.
Arguments:
- mass_per_volume: float32 [512, 64, 128], P('blk', 'grp'), may hold values from 0.5 to 2
- flow_vector: float32 [3, 512, 64, 128], P(None, 'blk', 'grp'), may hold values from -4 to 4
- magnetic_vector: float32 [3, 512, 64, 128], P(None, 'blk', 'grp'), may hold values from -4 to 4
- thermal_push: float32 [512, 64, 128], P('blk', 'grp'), may hold values from 1 to 4
- gradient_clipping_flags: int32 [512, 64, 128], P('blk', 'grp'), may hold values 0 or 1
- tracer_launch_volume: int32 [65536, 1], P(('grp', 'blk')), may hold values from 0 to 32767
- tracer_holder_tile: int32 [65536, 1], P(('grp', 'blk')), may hold values from 0 to 31; in each aligned block of 512 rows (0 to 511, 512 to 1023, ...) at most 32 rows name the same one
- holder_local_offset: int32 [65536, 1], P(('grp', 'blk')), may hold values from 0 to 1023
- neutral_thermal_field: float32 [50, 64, 512], P(None, 'blk'), may hold values from 0.5 to 2
- electric_voltage: float32 [64, 512], P('blk'), may hold values from -4 to 4
- reciprocal_operators: float32 [8, 50, 50], replicated, may hold values from 0 to 1
- warming_by_height: float32 [50], replicated, may hold values from 0.005 to 0.05
- pedersen_by_height: float32 [50], replicated, may hold values from 0.005 to 0.02
Outputs:
- conserved_quantities: float32 [8, 512, 64, 128], P(None, 'blk', 'grp')
- ending_thermal_state: float32 [50, 64, 512], P(None, 'blk', 'grp')
- ending_electric_voltage: float32 [64, 512], P('blk', 'grp')
The draws below stay inside these ranges and needn't reach their ends.
Inputs may be any that keep to these rules, and one draw needn't show every extreme that they name: `tracer_holder_tile`: among the 512 lines of one device at most 32 name the same owner. `tracer_launch_volume`: a cell of the sending device's own region. `holder_local_offset`: lon * 512 + lat inside the owner's 2 longitudes.
All inputs are finite; a program needn't handle non-finite values. No bound on the sum of `gradient_clipping_flags` on one device may be relied on, other than what follows from the above.
Results may differ from the reference program's by a relative error of at most 0.0003.
Values sent between devices are 32-bit elements; how exact they have to be, the bound alone decides.
No kernel may reach another device: no remote copies, remote signals or barrier semaphores. Data moves between devices by JAX's collectives and lax.ppermute only.
A program may use at most 128 MiB of HBM per device.

```python
import math
import jax
import jax.numpy as jnp
import numpy as np
from jax import lax

CX = 16
CY = 16
CZ = 128
SUBSTEPS = 2
COUPLINGS = 2
LINES_DEV = 512
HEIGHT_TIERS = 50
PARALLEL_NUMBER = 512
LON_DEV = 2
NBAND = 8
SWEEPS = 4
NX = 512
NY = 64
NZ = 128
MERIDIAN_NUMBER = 64
LINES = 65536
CAP = 32
N_BLK = 32


def draw_reciprocal_operators(key, part):
    key_diagonal = jax.random.fold_in(key, 11)
    key_spread = jax.random.fold_in(key, 23)
    diagonal = jax.random.uniform(key_diagonal, (NBAND, HEIGHT_TIERS), jnp.float32, 0.5, 1.0)
    spread = jax.random.uniform(key_spread, (NBAND, HEIGHT_TIERS, HEIGHT_TIERS), jnp.float32, 0.0, 0.01)
    identity = jnp.eye(HEIGHT_TIERS, dtype=jnp.float32)
    return spread * (1.0 - identity)[None] + diagonal[:, :, None] * identity[None]


def place_ends(array, own_key, low, top_value):
    extent = array.shape
    index_at = [jax.random.randint(jax.random.fold_in(own_key, axis), (), 0, extent[axis]) for axis in range(len(extent))]
    array = array.at[tuple(index_at)].set(low)
    longest = extent.index(max(extent))
    index_at[longest] = (index_at[longest] + 1) % extent[longest]
    return array.at[tuple(index_at)].set(top_value)


def level_of(stream_key, extent, shards, smallest, top_value):
    gain, own = 1.0, jax.random.fold_in(stream_key, 6)
    for axis_at, shards_of in shards:
        heights = jnp.exp(jax.random.uniform(jax.random.fold_in(own, axis_at), (shards_of,), jnp.float32, smallest / len(shards), top_value / len(shards)))
        gain = gain * jnp.repeat(heights, extent[axis_at] // shards_of).reshape([-1 if axis == axis_at else 1 for axis in range(len(extent))])
    return gain


def shared_out(rng, own, number, rows, number_of, top, most, lean):
    order = jax.random.permutation(rng, number_of)
    crowded, common = load_shares(number_of, rows * top, most, lean, True), load_shares(number_of, rows * top, most, lean, False)
    places = jnp.arange(number_of)

    def named(lengths, rotation):
        used = int((lengths > 0).sum())
        fixed = max(1, used // 4)
        shifted = fixed + (places - fixed + rotation * (used - fixed)) % max(1, number_of - fixed)
        return jnp.zeros((number_of,), jnp.int32).at[order[jnp.where(places < fixed, places, shifted)]].set(jnp.asarray(lengths, jnp.int32))

    lengths = jnp.where(number % 4 == 0, named(crowded, number // 4), named(common, number - number // 4 - 1))
    mixed = jax.random.permutation(jax.random.fold_in(own, 3), number_of)
    giver, taker = mixed[0:number_of // 2 * 2:2], mixed[1:number_of // 2 * 2:2]
    margin = jnp.minimum(lengths[giver] - 1, most - lengths[taker]) // 2
    margin = jnp.where((giver == order[0]) | (taker == order[0]) | (lengths[taker] == 0), 0, jnp.maximum(margin, 0))
    shifted = jax.random.randint(jax.random.fold_in(own, 4), (number_of // 2,), 0, 1 << 20) % (margin + 1)
    lengths = lengths.at[giver].add(-shifted).at[taker].add(shifted)
    labels = jnp.searchsorted(jnp.cumsum(lengths), jnp.arange(rows * top), side="right").astype(jnp.int32)
    grid = labels.reshape(top, rows).T
    grid = grid[jax.random.permutation(jax.random.fold_in(own, 1), rows)]
    rotation = jax.random.randint(jax.random.fold_in(own, 2), (rows, 1), 0, top)
    return jnp.take_along_axis(grid, (jnp.arange(top)[None, :] + rotation) % top, axis=1)


def load_shares(count, total, reach, lean, full):
    loads = [(1 << 20) // math.isqrt(rank ** lean) + 1 for rank in range(1, count + 1)]
    largest = reach if full else min(reach, max(-(-total // count), total * loads[0] // sum(loads)))
    least = 1 if total - largest >= count - 1 else 0
    given, surplus = [largest] + [least] * (count - 1), total - largest - least * (count - 1)
    while surplus > 0:
        candidates = [i for i in range(1, count) if given[i] < largest] or [i for i in range(1, count) if given[i] < reach]
        mass, budget = sum([loads[i] for i in candidates]), surplus
        for i in candidates:
            extra = min(reach - given[i], max(1, budget * loads[i] // mass), surplus)
            given[i] = given[i] + extra
            surplus = surplus - extra
    return np.array(given)


def gaussian(key, shape, scale, reach, cuts=(), held_as=jnp.bfloat16):
    drawn = scale * jax.random.normal(key, shape, jnp.float32)
    if cuts:
        drawn = drawn * level_of(key, shape, cuts, -0.22, 0.18)
    return jnp.clip(drawn, -reach, reach).astype(held_as)


def setup_inputs(seed: int = 0) -> dict:
    key_of = jax.random.split(jax.random.key(seed), 14)
    mass_per_volume = jnp.clip(jnp.exp(math.log(2.0) - 1.3862944 * jax.random.uniform(key_of[0], (NX, NY, NZ), jnp.float32) ** level_of(key_of[0], (NX, NY, NZ), ((0, 32), (1, 4)), -0.2, 0.2)), 0.5, 2.0)
    flow_vector = gaussian(key_of[1], (3, NX, NY, NZ), 0.3, 4.0, ((1, 32), (2, 4)), jnp.float32)
    magnetic_vector = gaussian(key_of[2], (3, NX, NY, NZ), 0.5, 4.0, ((1, 32), (2, 4)), jnp.float32)
    thermal_push = jnp.clip(jnp.exp(math.log(4.0) - 1.3862944 * jax.random.uniform(key_of[3], (NX, NY, NZ), jnp.float32) ** level_of(key_of[3], (NX, NY, NZ), ((0, 32), (1, 4)), -0.2, 0.2)), 1.0, 4.0)
    gradient_clipping_flags = place_ends((jax.random.randint(key_of[4], (NX, NY, NZ), 0, 2) < 1).astype(jnp.int32), jax.random.fold_in(key_of[4], 1), 0, 1)
    tracer_launch_volume = place_ends(jax.random.randint(key_of[5], (LINES, 1), 0, CX * CY * CZ), jax.random.fold_in(key_of[5], 1), 0, (CX * CY * CZ) - 1).astype(jnp.int32)
    tracer_holder_tile_keys = jax.random.split(jax.random.fold_in(key_of[6], 1), LINES // LINES_DEV)
    tracer_holder_tile_turns = jax.random.permutation(jax.random.fold_in(key_of[6], 3), LINES // LINES_DEV)
    tracer_holder_tile = jax.vmap(lambda own, number: shared_out(jax.random.fold_in(key_of[6], 2), own, number, LINES_DEV, N_BLK, 1, CAP, 2))(tracer_holder_tile_keys, tracer_holder_tile_turns).reshape((LINES, 1))
    holder_local_offset = place_ends(jax.random.randint(key_of[7], (LINES, 1), 0, LON_DEV * PARALLEL_NUMBER), jax.random.fold_in(key_of[7], 1), 0, (LON_DEV * PARALLEL_NUMBER) - 1).astype(jnp.int32)
    neutral_thermal_field = jnp.clip(jnp.exp(math.log(2.0) - 1.3862944 * jax.random.uniform(key_of[8], (HEIGHT_TIERS, MERIDIAN_NUMBER, PARALLEL_NUMBER), jnp.float32) ** level_of(key_of[8], (HEIGHT_TIERS, MERIDIAN_NUMBER, PARALLEL_NUMBER), ((1, 32),), -0.2, 0.2)), 0.5, 2.0)
    electric_voltage = gaussian(key_of[9], (MERIDIAN_NUMBER, PARALLEL_NUMBER), 0.5, 4.0, ((0, 32),), jnp.float32)
    reciprocal_operators = draw_reciprocal_operators(jax.random.fold_in(key_of[13], 71), 0)
    warming_by_height = jnp.clip(jnp.exp(jax.random.uniform(key_of[11], (HEIGHT_TIERS,), jnp.float32, math.log(0.005), math.log(0.05))), 0.005, 0.05)
    pedersen_by_height = jnp.clip(jnp.exp(jax.random.uniform(key_of[12], (HEIGHT_TIERS,), jnp.float32, math.log(0.005), math.log(0.02))), 0.005, 0.02)
    return dict(mass_per_volume=mass_per_volume, flow_vector=flow_vector, magnetic_vector=magnetic_vector, thermal_push=thermal_push, gradient_clipping_flags=gradient_clipping_flags, tracer_launch_volume=tracer_launch_volume, tracer_holder_tile=tracer_holder_tile, holder_local_offset=holder_local_offset, neutral_thermal_field=neutral_thermal_field, electric_voltage=electric_voltage, reciprocal_operators=reciprocal_operators, warming_by_height=warming_by_height, pedersen_by_height=pedersen_by_height)


HEAT_RATIO = 5.0 / 3.0
TIME_STEP = 0.02
DRAG_RATE = 0.5

def to_conserved(fluid):
    mass_per_volume = fluid[0]
    flow_vector = fluid[1:4]
    magnetic_vector = fluid[4:7]
    thermal_push = fluid[7]
    energy = thermal_push / (HEAT_RATIO - 1.0) + 0.5 * mass_per_volume * lax.optimization_barrier(jnp.sum(flow_vector * flow_vector, axis=0)) + 0.5 * lax.optimization_barrier(jnp.sum(magnetic_vector * magnetic_vector, axis=0))
    return jnp.concatenate([mass_per_volume[None], mass_per_volume[None] * flow_vector, magnetic_vector, energy[None]], axis=0)

def to_primitive(conserved_quantities):
    mass_per_volume = conserved_quantities[0]
    momentum = conserved_quantities[1:4]
    magnetic_vector = conserved_quantities[4:7]
    thermal_push = (HEAT_RATIO - 1.0) * (conserved_quantities[7] - 0.5 * lax.optimization_barrier(jnp.sum(momentum * momentum, axis=0)) / mass_per_volume - 0.5 * lax.optimization_barrier(jnp.sum(magnetic_vector * magnetic_vector, axis=0)))
    return jnp.concatenate([mass_per_volume[None], momentum / mass_per_volume[None], magnetic_vector, thermal_push[None]], axis=0)

def physical_flux(fluid, direction):
    mass_per_volume = fluid[0]
    flow_vector = fluid[1:4]
    magnetic_vector = fluid[4:7]
    thermal_push = fluid[7]
    shape = (3,) + (1,) * (fluid.ndim - 1)
    normal = (jnp.arange(3) == direction).astype(jnp.float32).reshape(shape)
    normal_speed = flow_vector[direction]
    normal_field = magnetic_vector[direction]
    field_square = lax.optimization_barrier(jnp.sum(magnetic_vector * magnetic_vector, axis=0))
    across = lax.optimization_barrier(jnp.sum(magnetic_vector * magnetic_vector * (1.0 - normal), axis=0))
    total_pressure = thermal_push + 0.5 * field_square
    energy = thermal_push / (HEAT_RATIO - 1.0) + 0.5 * mass_per_volume * lax.optimization_barrier(jnp.sum(flow_vector * flow_vector, axis=0)) + 0.5 * field_square
    mass_flux = mass_per_volume * normal_speed
    momentum_flux = mass_per_volume * flow_vector * normal_speed - normal_field * magnetic_vector + total_pressure * normal
    field_flux = normal_speed * magnetic_vector - normal_field * flow_vector
    energy_flux = (energy + total_pressure) * normal_speed - normal_field * lax.optimization_barrier(jnp.sum(flow_vector * magnetic_vector, axis=0))
    flux = jnp.concatenate([mass_flux[None], momentum_flux, field_flux, energy_flux[None]], axis=0)
    conserved_quantities = jnp.concatenate([mass_per_volume[None], mass_per_volume[None] * flow_vector, magnetic_vector, energy[None]], axis=0)
    sound = HEAT_RATIO * thermal_push / mass_per_volume
    alfven = field_square / mass_per_volume
    transverse = across / mass_per_volume
    fast = 0.5 * (sound + alfven + jnp.sqrt((sound - alfven) ** 2 + 4.0 * sound * transverse))
    return (flux, conserved_quantities, jnp.abs(normal_speed) + jnp.sqrt(fast))

def face_flux(left, right, direction):
    flux_left, state_left, speed_left = physical_flux(left, direction)
    flux_right, state_right, speed_right = physical_flux(right, direction)
    return 0.5 * (flux_left + flux_right) - 0.5 * jnp.maximum(speed_left, speed_right)[None] * (state_right - state_left)

def limited(forward, backward):
    return 0.5 * (jnp.sign(forward) + jnp.sign(backward)) * jnp.minimum(jnp.abs(forward), jnp.abs(backward))

def rolled_divergence(fluid, limiter, axis):
    forward = jnp.roll(fluid, -1, axis) - fluid
    slope = limited(forward, jnp.roll(forward, 1, axis)) * limiter[None]
    left = fluid + 0.5 * slope
    right = jnp.roll(fluid - 0.5 * slope, -1, axis)
    flux = face_flux(left, right, axis - 1)
    return flux - jnp.roll(flux, 1, axis)

def vertical_tridiagonal_update(neutral_thermal_field, warming_speed, warming_by_height, reciprocal_operators):
    forcing_vector_combined = neutral_thermal_field + warming_by_height[:, None, None] * warming_speed[None]
    levels, longs, lats = forcing_vector_combined.shape
    bands = reciprocal_operators.shape[0]
    grouped = forcing_vector_combined.reshape(levels, longs, bands, lats // bands)
    solved = jnp.einsum('bzy,ylbk->zlbk', reciprocal_operators, grouped, precision=lax.Precision.HIGHEST)
    return solved.reshape(levels, longs, lats)

def relax(extended, source):
    integrated_pedersen = extended[0]
    electric_voltage = extended[1]
    centre = integrated_pedersen[1:-1, 1:-1]
    east = 0.5 * (centre + integrated_pedersen[2:, 1:-1])
    west = 0.5 * (centre + integrated_pedersen[:-2, 1:-1])
    north = 0.5 * (centre + integrated_pedersen[1:-1, 2:])
    south = 0.5 * (centre + integrated_pedersen[1:-1, :-2])
    total = east * electric_voltage[2:, 1:-1] + west * electric_voltage[:-2, 1:-1] + north * electric_voltage[1:-1, 2:] + south * electric_voltage[1:-1, :-2]
    return (total - source) / (east + west + north + south)

def grid_margin(integrated_pedersen, electric_voltage):
    stacked = jnp.stack([integrated_pedersen, electric_voltage], axis=0)
    wrapped = jnp.concatenate([stacked[:, -1:], stacked, stacked[:, :1]], axis=1)
    return jnp.pad(wrapped, ((0, 0), (0, 0), (1, 1)))

def apply_drag(conserved_quantities, cells, line_potential, line_conductance):
    flat = conserved_quantities.reshape(conserved_quantities.shape[0], -1)
    push = DRAG_RATE * line_conductance * (flat[0][cells] * line_potential - flat[2][cells])
    added = jax.ops.segment_sum(push, cells, num_segments=flat.shape[1])
    new_energy = flat[7] + (flat[2] * added + 0.5 * added * added) / flat[0]
    flat = flat.at[2].set(flat[2] + added).at[7].set(new_energy)
    return flat.reshape(conserved_quantities.shape)

def reference(mass_per_volume, flow_vector, magnetic_vector, thermal_push, gradient_clipping_flags, tracer_launch_volume, tracer_holder_tile, holder_local_offset, neutral_thermal_field, electric_voltage, reciprocal_operators, warming_by_height, pedersen_by_height):
    limiter = gradient_clipping_flags.astype(jnp.float32)
    fluid = jnp.concatenate([mass_per_volume[None], flow_vector, magnetic_vector, thermal_push[None]], axis=0)
    device = (jnp.arange(LINES, dtype=jnp.int32) // LINES_DEV).astype(jnp.int32)
    grp_index = device // N_BLK
    blk_index = device % N_BLK
    local = tracer_launch_volume[:, 0].astype(jnp.int32)
    cell_x = blk_index * CX + local // (CY * CZ)
    cell_y = grp_index * CY + local // CZ % CY
    cells = ((cell_x * NY + cell_y) * NZ + local % CZ).astype(jnp.int32)
    within = holder_local_offset[:, 0].astype(jnp.int32)
    columns = ((tracer_holder_tile[:, 0] * LON_DEV + within // PARALLEL_NUMBER) * PARALLEL_NUMBER + within % PARALLEL_NUMBER).astype(jnp.int32)
    conserved_quantities = to_conserved(fluid)
    for coupling in range(COUPLINGS):
        field_x = fluid[4]
        field_y = fluid[5]
        current = 0.5 * (jnp.roll(field_y, -1, 0) - jnp.roll(field_y, 1, 0)) - 0.5 * (jnp.roll(field_x, -1, 1) - jnp.roll(field_x, 1, 1))
        precipitation = fluid[7] * jnp.sqrt(fluid[7] / fluid[0])
        values = jnp.stack([current.reshape(-1)[cells], precipitation.reshape(-1)[cells]], axis=1)
        deposit = jax.ops.segment_sum(values, columns, num_segments=MERIDIAN_NUMBER * PARALLEL_NUMBER)
        jsum = deposit[:, 0].reshape(MERIDIAN_NUMBER, PARALLEL_NUMBER)
        warming_accumulated = deposit[:, 1].reshape(MERIDIAN_NUMBER, PARALLEL_NUMBER)
        for substep in range(SUBSTEPS):
            conserved_quantities = to_conserved(fluid) - TIME_STEP * (rolled_divergence(fluid, limiter, 1) + rolled_divergence(fluid, limiter, 2) + rolled_divergence(fluid, limiter, 3))
            if substep + 1 < SUBSTEPS:
                fluid = to_primitive(conserved_quantities)
        neutral_thermal_field = vertical_tridiagonal_update(neutral_thermal_field, warming_accumulated, warming_by_height, reciprocal_operators)
        integrated_pedersen = jnp.einsum('k,krb->rb', pedersen_by_height, neutral_thermal_field, precision=lax.Precision.HIGHEST)
        for sweep in range(SWEEPS):
            electric_voltage = relax(grid_margin(integrated_pedersen, electric_voltage), jsum)
        line_potential = electric_voltage.reshape(-1)[columns]
        line_conductance = integrated_pedersen.reshape(-1)[columns]
        conserved_quantities = apply_drag(conserved_quantities, cells, line_potential, line_conductance)
        fluid = to_primitive(conserved_quantities)
    return (conserved_quantities, neutral_thermal_field, electric_voltage)
```

```python
import functools

import jax
import jax.numpy as jnp
from jax import lax
from jax.experimental import pallas as pl
from jax.experimental.pallas import tpu as pltpu
from jax.sharding import PartitionSpec as P

SWEEPS = 4
HEAT_RATIO = 5.0 / 3.0
TIME_STEP = 0.02
DRAG_RATE = 0.5
CX = 16
CY = 16
CZ = 128
BLOCKS = 32
CAP = 32
SLOTS = BLOCKS * CAP
LATS = 512
BANDS = 8
F32 = jnp.float32
BF16 = jnp.bfloat16
HIGHEST = lax.Precision.HIGHEST
VMEM_LIMIT = 40 * 1024 * 1024


def shape(*dims):
    return jax.ShapeDtypeStruct(dims, F32)


def kernel_call(body, outs, microseconds, scratch=()):
    return pl.pallas_call(
        body,
        out_shape=outs,
        scratch_shapes=list(scratch),
        compiler_params=pltpu.CompilerParams(vmem_limit_bytes=VMEM_LIMIT),
        cost_estimate=pl.CostEstimate(
            flops=0, bytes_accessed=int(microseconds * 3.3e6), transcendentals=0
        ),
    )


def half_slope(before, centre, after, half_limiter):
    forward = after - centre
    backward = centre - before
    low = jnp.minimum(forward, backward)
    high = jnp.maximum(forward, backward)
    return half_limiter * (jnp.maximum(low, 0.0) + jnp.minimum(high, 0.0))


def side(w, d):
    rho, ux, uy, uz, bx, by, bz, p = w
    u = (ux, uy, uz)
    b = (bx, by, bz)
    e, f = [k for k in range(3) if k != d]
    inverse = 1.0 / rho
    m = [rho * c for c in u]
    across = b[e] * b[e] + b[f] * b[f]
    square = across + b[d] * b[d]
    kinetic = m[0] * ux + m[1] * uy + m[2] * uz
    total = p + 0.5 * square
    energy = 1.5 * p + 0.5 * (kinetic + square)
    along = ux * bx + uy * by + uz * bz
    flux = [None] * 8
    flux[0] = m[d]
    for k in range(3):
        flux[1 + k] = m[k] * u[d] - b[d] * b[k]
        if k != d:
            flux[4 + k] = u[d] * b[k] - b[d] * u[k]
    flux[1 + d] = flux[1 + d] + total
    flux[7] = (energy + total) * u[d] - b[d] * along
    sound = (HEAT_RATIO * p) * inverse
    alfven = square * inverse
    transverse = across * inverse
    gap = sound - alfven
    fast = 0.5 * (sound + alfven + jnp.sqrt(gap * gap + 4.0 * sound * transverse))
    speed = jnp.abs(u[d]) + jnp.sqrt(fast)
    return flux, [rho, m[0], m[1], m[2], bx, by, bz, energy], speed


def face_flux(left, right, d):
    flux_l, state_l, speed_l = side(left, d)
    flux_r, state_r, speed_r = side(right, d)
    speed = 0.5 * jnp.maximum(speed_l, speed_r)
    out = []
    for k in range(8):
        jump = speed * (state_r[k] - state_l[k])
        if flux_l[k] is None:
            out.append(-jump)
        else:
            out.append(0.5 * (flux_l[k] + flux_r[k]) - jump)
    return out


def substep_kernel(mode, split, refs):
    refs = list(refs)
    w_ref, lim_ref = refs[:2]
    faces = refs[2:6]
    lims = refs[6:10]
    refs = refs[10:]
    if split:
        uy_ref = refs[0]
        uy_faces = refs[1:5]
        refs = refs[5:]
    if mode == "final":
        push_ref = refs[0]
        refs = refs[1:]
        out_ref = refs[0]
        outs = ()
        refs = refs[1:]
    else:
        out_ref = refs[0]
        outs = refs[1:9]
        refs = refs[9:]
    ext, lim_ext, lx, hx, lb, ht = refs
    iota = lax.broadcasted_iota(jnp.int32, (CY, CZ), 0)
    first_row = iota == 0
    last_row = iota == CY - 1

    def halo(which, f, r):
        if split:
            if f == 2:
                return uy_faces[which][r]
            f = f if f < 2 else f - 1
        return faces[which][2 * f + r]

    for f in range(8):
        ext[f, 0] = halo(2, f, 0)
        ext[f, 1] = halo(2, f, 1)
        if split and f == 2:
            ext[f, 2 : 2 + CX] = uy_ref[...]
        else:
            ext[f, 2 : 2 + CX] = w_ref[f]
        ext[f, 2 + CX] = halo(3, f, 0)
        ext[f, 3 + CX] = halo(3, f, 1)
    lim_ext[0] = 0.5 * lims[2][...]
    lim_ext[1 : 1 + CX] = 0.5 * lim_ref[...]
    lim_ext[1 + CX] = 0.5 * lims[3][...]

    def row(f, r):
        return ext[f, 2 : 2 + CX, r, :]

    lim_low = 0.5 * lims[0][...]
    lim_high = 0.5 * lims[1][...]
    lim_last = lim_ext[1 : 1 + CX, CY - 1, :]
    left = []
    right = []
    for f in range(8):
        low0, low1 = halo(0, f, 0), halo(0, f, 1)
        high0, high1 = halo(1, f, 0), halo(1, f, 1)
        lb[f] = low1 + half_slope(low0, low1, row(f, 0), lim_low)
        last = row(f, CY - 1)
        left.append(last + half_slope(row(f, CY - 2), last, high0, lim_last))
        right.append(high0 - half_slope(last, high0, high1, lim_high))
    for f, value in enumerate(face_flux(left, right, 1)):
        ht[f] = value

    left = []
    right = []
    for f in range(8):
        a, b, c, d = ext[f, 0], ext[f, 1], ext[f, 2], ext[f, 3]
        left.append(b + half_slope(a, b, c, lim_ext[0]))
        s = half_slope(b, c, d, lim_ext[1])
        right.append(c - s)
        lx[f] = c + s
    for f, value in enumerate(face_flux(left, right, 0)):
        hx[f] = value

    def plane(i, carry):
        lim = lim_ext[i + 1]
        lim_next = lim_ext[i + 2]
        w = [ext[f, i + 2] for f in range(8)]
        left = [lx[f] for f in range(8)]
        right = []
        for f in range(8):
            after = ext[f, i + 3]
            s = half_slope(w[f], after, ext[f, i + 4], lim_next)
            right.append(after - s)
            lx[f] = after + s
        flux = face_flux(left, right, 0)
        total = []
        for f in range(8):
            total.append(flux[f] - hx[f])
            hx[f] = flux[f]
        left = []
        right = []
        for f in range(8):
            before = jnp.where(first_row, halo_row(f, i, 1), pltpu.roll(w[f], 1, 0))
            after = jnp.where(last_row, halo_row(f, i, 2), pltpu.roll(w[f], CY - 1, 0))
            s = half_slope(before, w[f], after, lim)
            right.append(w[f] - s)
            left.append(
                jnp.where(first_row, lb[f, pl.ds(i, 1), :], pltpu.roll(w[f] + s, 1, 0))
            )
        flux = face_flux(left, right, 1)
        for f in range(8):
            upper = jnp.where(
                last_row, ht[f, pl.ds(i, 1), :], pltpu.roll(flux[f], CY - 1, 0)
            )
            total[f] = total[f] + (upper - flux[f])
        left = []
        right = []
        for f in range(8):
            s = half_slope(pltpu.roll(w[f], 1, 1), w[f], pltpu.roll(w[f], CZ - 1, 1), lim)
            left.append(w[f] + s)
            right.append(pltpu.roll(w[f] - s, CZ - 1, 1))
        flux = face_flux(left, right, 2)
        for f in range(8):
            total[f] = total[f] + (flux[f] - pltpu.roll(flux[f], 1, 1))
        rho, ux, uy, uz, bx, by, bz, p = w
        m = [rho * ux, rho * uy, rho * uz]
        energy = 1.5 * p + 0.5 * (
            m[0] * ux + m[1] * uy + m[2] * uz + bx * bx + by * by + bz * bz
        )
        state = [rho, m[0], m[1], m[2], bx, by, bz, energy]
        state = [state[f] - TIME_STEP * total[f] for f in range(8)]
        rho, mx, my, mz, bx, by, bz, energy = state
        if mode == "final":
            added = rho * push_ref[0, i] - my * push_ref[1, i]
            energy = energy + (my * added + 0.5 * added * added) / rho
            result = [rho, mx, my + added, mz, bx, by, bz, energy]
        else:
            inverse = 1.0 / rho
            p = (HEAT_RATIO - 1.0) * (
                energy
                - 0.5 * (mx * mx + my * my + mz * mz) * inverse
                - 0.5 * (bx * bx + by * by + bz * bz)
            )
            result = [rho, mx * inverse, my * inverse, mz * inverse, bx, by, bz, p]
        for f in range(8):
            out_ref[f, i] = result[f]
        return carry

    def halo_row(f, i, which):
        if split and f == 2:
            return uy_faces[0][1, pl.ds(i, 1), :] if which == 1 else uy_faces[1][0, pl.ds(i, 1), :]
        g = (f if f < 2 else f - 1) if split else f
        if which == 1:
            return faces[0][2 * g + 1, pl.ds(i, 1), :]
        return faces[1][2 * g, pl.ds(i, 1), :]

    lax.fori_loop(0, CX, plane, 0)
    if mode != "final":
        write_faces(out_ref, outs, mode == "late")


def write_faces(w_ref, outs, late):
    y_low, y_high, x_low, x_high, bx_low, bx_high, by_low, by_high = outs
    fields = [f for f in range(8) if not (late and f == 2)]
    for g, f in enumerate(fields):
        for r in range(2):
            y_low[2 * g + r] = w_ref[f, :, r, :]
            y_high[2 * g + r] = w_ref[f, :, CY - 2 + r, :]
            x_low[2 * g + r] = w_ref[f, r]
            x_high[2 * g + r] = w_ref[f, CX - 2 + r]
    bx_low[...] = w_ref[4, :, 0, :]
    bx_high[...] = w_ref[4, :, CY - 1, :]
    by_low[...] = w_ref[5, 0]
    by_high[...] = w_ref[5, CX - 1]


def face_shapes(fields):
    return [shape(2 * fields, CX, CZ)] * 4 + [shape(CX, CZ)] * 4


def pack_kernel(rho, u, b, p, flags, w_ref, lim_ref, *outs):
    w_ref[0] = rho[...]
    w_ref[1:4] = u[...]
    w_ref[4:7] = b[...]
    w_ref[7] = p[...]
    lim_ref[...] = flags[...].astype(F32)
    faces, lims = outs[:8], outs[8:]
    write_faces(w_ref, faces, False)
    lims[0][...] = lim_ref[:, 0, :]
    lims[1][...] = lim_ref[:, CY - 1, :]
    lims[2][...] = lim_ref[0]
    lims[3][...] = lim_ref[CX - 1]


def substep(mode, split, args):
    scratch = [
        pltpu.VMEM((8, CX + 4, CY, CZ), F32),
        pltpu.VMEM((CX + 2, CY, CZ), F32),
        pltpu.VMEM((8, CY, CZ), F32),
        pltpu.VMEM((8, CY, CZ), F32),
        pltpu.VMEM((8, CX, CZ), F32),
        pltpu.VMEM((8, CX, CZ), F32),
    ]
    outs = [shape(8, CX, CY, CZ)]
    if mode == "all":
        outs += face_shapes(8)
    elif mode == "late":
        outs += face_shapes(7)

    def body(*refs):
        substep_kernel(mode, split, refs)

    return kernel_call(body, outs, 5.0, scratch)(*args)


def rounded_parts(value, count):
    parts = []
    for _ in range(count):
        part = value.astype(BF16).astype(F32)
        parts.append(part)
        value = value - part
    return parts


def one_hot(positions, extent):
    rows = lax.broadcasted_iota(jnp.int32, (extent, SLOTS), 0)
    return rows == positions.astype(jnp.int32)


def spread(rows, out_ref):
    for t in range(SLOTS // CZ):
        tile = rows[:, t * CZ : (t + 1) * CZ]
        for j in range(CZ // CAP):
            moved = tile if j == 0 else pltpu.roll(tile, CZ - CAP * j, 1)
            out_ref[t * (CZ // CAP) + j] = moved[0:4]


def collect(block_ref, rows_ref):
    lane = lax.broadcasted_iota(jnp.int32, (8, CZ), 1) // CAP
    per = CZ // CAP
    for t in range(SLOTS // CZ):
        total = jnp.zeros((8, CZ), F32)
        for j in range(per):
            block = block_ref[t * per + j]
            block = jnp.concatenate([block, block], axis=0)
            moved = block if j == 0 else pltpu.roll(block, CAP * j, 1)
            total = jnp.where(lane == j, moved, total)
        rows_ref[:, t * CZ : (t + 1) * CZ] = total


def slot_kernel(owner_ref, rows_ref, out_ref):
    count = owner_ref.shape[0]
    owner = owner_ref[...]
    others = rows_ref[4:5, :].astype(jnp.int32)
    here = lax.broadcasted_iota(jnp.int32, (count, count), 0)
    there = lax.broadcasted_iota(jnp.int32, (count, count), 1)
    earlier = jnp.where((owner == others) & (there < here), 1.0, 0.0)
    rank = jnp.sum(earlier, axis=1, keepdims=True)
    slot = owner * CAP + rank.astype(jnp.int32)
    lanes = lax.broadcasted_iota(jnp.int32, (count, SLOTS), 1)
    table = jnp.where(lanes == slot, 1.0, 0.0).astype(BF16)
    found = jnp.dot(rows_ref[...].astype(BF16), table, preferred_element_type=F32)
    out_ref[...] = found
    out_ref[0:1, :] = found[0:1] + found[5:6] - 1.0
    out_ref[2:3, :] = found[2:3] * CZ + found[3:4]


def payload_kernel(w_ref, bx_low, bx_high, by_low, by_high, slot_ref, out_ref, fields, rows):
    iota = lax.broadcasted_iota(jnp.int32, (CY, CZ), 0)
    for x in range(CX):
        east = by_high[...] if x == CX - 1 else w_ref[5, x + 1]
        west = by_low[...] if x == 0 else w_ref[5, x - 1]
        bx = w_ref[4, x]
        north = jnp.where(iota == CY - 1, bx_high[x : x + 1, :], pltpu.roll(bx, CY - 1, 0))
        south = jnp.where(iota == 0, bx_low[x : x + 1, :], pltpu.roll(bx, 1, 0))
        p = w_ref[7, x]
        fields[x * CY : (x + 1) * CY, 0:CZ] = 0.5 * (east - west) - 0.5 * (north - south)
        fields[x * CY : (x + 1) * CY, CZ : 2 * CZ] = p * jnp.sqrt(p / w_ref[0, x])
    cells = one_hot(slot_ref[0:1, :], CX * CY).astype(F32).astype(BF16)
    levels = one_hot(slot_ref[1:2, :], CZ)
    across = fields[...].T
    found = jnp.zeros((2 * CZ, SLOTS), F32)
    for part in rounded_parts(across, 3):
        found = found + jnp.dot(part.astype(BF16), cells, preferred_element_type=F32)
    rows[...] = slot_ref[...]
    for v in range(2):
        kept = jnp.where(levels, found[v * CZ : (v + 1) * CZ], 0.0)
        rows[v : v + 1, :] = jnp.sum(kept, axis=0, keepdims=True)
    spread(rows[...], out_ref)


def deposit(rows, column, out_ref, stack):
    upper = column >= float(LATS)
    place = one_hot(jnp.where(upper, column - LATS, column), LATS).astype(F32).astype(BF16)
    for v in range(2):
        for lon in range(2):
            kept = jnp.where(upper == (lon == 1), rows[v : v + 1, :], 0.0)
            for k, part in enumerate(rounded_parts(kept, 3)):
                at = 4 * k + 2 * v + lon
                stack[at : at + 1, :] = part
    stack[12:16, :] = jnp.zeros((4, SLOTS), F32)
    total = lax.dot_general(
        stack[...].astype(BF16), place, (((1,), (1,)), ((), ())), preferred_element_type=F32
    )
    out_ref[...] = total[0:4] + total[4:8] + total[8:12]


def deposit_first_kernel(block_ref, out_ref, column_ref, rows, stack):
    collect(block_ref, rows)
    column_ref[...] = rows[...]
    deposit(rows[...], rows[2:3, :], out_ref, stack)


def deposit_next_kernel(block_ref, column_ref, out_ref, rows, stack):
    collect(block_ref, rows)
    deposit(rows[...], column_ref[2:3, :], out_ref, stack)


def scatter(block_ref, slot_ref, rows, parts):
    collect(block_ref, rows)
    weight = DRAG_RATE * rows[1:2, :]
    cells = one_hot(slot_ref[0:1, :], CX * CY).astype(F32).astype(BF16)
    levels = one_hot(slot_ref[1:2, :], CZ)
    for v, value in enumerate((weight * rows[0:1, :], weight)):
        for k, part in enumerate(rounded_parts(value, 2)):
            at = (2 * v + k) * CZ
            parts[at : at + CZ, :] = jnp.where(levels, part, 0.0).astype(BF16)
    total = lax.dot_general(
        cells, parts[...], (((1,), (1,)), ((), ())), preferred_element_type=F32
    )
    first = total[:, 0:CZ] + total[:, CZ : 2 * CZ]
    second = total[:, 2 * CZ : 3 * CZ] + total[:, 3 * CZ :]
    return first.reshape(CX, CY, CZ), second.reshape(CX, CY, CZ)


def drag_kernel(block_ref, slot_ref, w_ref, out_ref, y_low, y_high, x_low, x_high, rows, parts):
    first, second = scatter(block_ref, slot_ref, rows, parts)
    out_ref[...] = w_ref[2] * (1.0 - second) + first
    for r in range(2):
        y_low[r] = out_ref[:, r, :]
        y_high[r] = out_ref[:, CY - 2 + r, :]
        x_low[r] = out_ref[r]
        x_high[r] = out_ref[CX - 2 + r]


def scatter_kernel(block_ref, slot_ref, out_ref, rows, parts):
    first, second = scatter(block_ref, slot_ref, rows, parts)
    out_ref[0] = first
    out_ref[1] = second


def base_kernel(inverse_ref, pedersen_ref, warming_ref, thermal_ref, out_ref, factors):
    levels = pedersen_ref.shape[0]
    for band in range(BANDS):
        factors[band : band + 1, :] = jnp.sum(
            pedersen_ref[...] * inverse_ref[band], axis=0, keepdims=True
        )
    once = factors[0:BANDS, :]
    for band in range(BANDS):
        twice = jnp.dot(once, inverse_ref[band], precision=HIGHEST, preferred_element_type=F32)
        factors[BANDS + band : BANDS + band + 1, :] = twice[band : band + 1, :]
    both = factors[...]
    lane_band = lax.broadcasted_iota(jnp.int32, (BANDS, LATS), 1) // (LATS // BANDS)
    own = lane_band == lax.broadcasted_iota(jnp.int32, (BANDS, LATS), 0)

    def pick(values):
        return jnp.sum(jnp.where(own, values, 0.0), axis=0, keepdims=True)

    for lon in range(2):
        field = thermal_ref[:, lon, :]
        found = jnp.dot(both, field, precision=HIGHEST, preferred_element_type=F32)
        out_ref[lon : lon + 1, :] = pick(found[0:BANDS])
        out_ref[2 + lon : 3 + lon, :] = pick(found[BANDS:])
    response = jnp.sum(both * warming_ref[...], axis=1, keepdims=True)
    out_ref[4:5, :] = pick(jnp.broadcast_to(response[0:BANDS], (BANDS, LATS)))
    out_ref[5:6, :] = pick(jnp.broadcast_to(response[BANDS:], (BANDS, LATS)))
    out_ref[6:8, :] = jnp.zeros((2, LATS), F32)


def gather_kernel(at, a, b, c, d, potential, base, out_ref):
    out_ref[0:4, :] = (a[...] + b[...]) + (c[...] + d[...])
    out_ref[4:6, :] = potential[...]
    out_ref[6:8, :] = base[at : at + 2, :]


def sweep_kernel(m2, m1, here, p1, p2, base, column_ref, out_v, out_block, out_base, ext, table):
    for k in range(4):
        for at, ref in enumerate((m2, m1, here, p1, p2)):
            ext[k, 2 * at : 2 * at + 2, :] = ref[2 * k : 2 * k + 2, :]
        ext[k, 10:16, :] = jnp.ones((6, LATS), F32)
    source = ext[0]
    heat = ext[1]
    potential = ext[2]
    conductance = ext[3] + base[4:5, :] * heat
    lane = lax.broadcasted_iota(jnp.int32, (16, LATS), 1)
    first = lane == 0
    last = lane == LATS - 1

    def up(v):
        return jnp.where(last, 0.0, pltpu.roll(v, LATS - 1, 1))

    def down(v):
        return jnp.where(first, 0.0, pltpu.roll(v, 1, 1))

    east = 0.5 * (conductance + pltpu.roll(conductance, 15, 0))
    west = 0.5 * (conductance + pltpu.roll(conductance, 1, 0))
    north = 0.5 * (conductance + up(conductance))
    south = 0.5 * (conductance + down(conductance))
    inverse = 1.0 / (east + west + north + south)
    for _ in range(SWEEPS):
        potential = (
            east * pltpu.roll(potential, 15, 0)
            + west * pltpu.roll(potential, 1, 0)
            + north * up(potential)
            + south * down(potential)
            - source
        ) * inverse
    ext[2] = potential
    ext[3] = conductance
    out_v[...] = ext[2, 4:6, :]
    out_base[...] = base[...]
    out_base[2:4, :] = base[2:4, :] + base[5:6, :] * here[2:4, :]
    for v in range(2):
        for k, part in enumerate(rounded_parts(ext[2 + v, 4:6, :], 3)):
            table[4 * k + 2 * v : 4 * k + 2 * v + 2, :] = part
    table[12:16, :] = jnp.zeros((4, LATS), F32)
    column = column_ref[2:3, :]
    upper = column >= float(LATS)
    place = one_hot(jnp.where(upper, column - LATS, column), LATS).astype(F32).astype(BF16)
    found = jnp.dot(table[...].astype(BF16), place, preferred_element_type=F32)
    found = found[0:4] + found[4:8] + found[8:12]
    voltage = jnp.where(upper, found[1:2], found[0:1])
    weight = jnp.where(upper, found[3:4], found[2:3])
    sub = lax.broadcasted_iota(jnp.int32, (8, SLOTS), 0)
    spread(jnp.where(sub == 0, voltage, weight), out_block)


def thermal_kernel(thermal_ref, inverse_ref, warming_ref, one_ref, two_ref, out_ref):
    low_band = lax.broadcasted_iota(jnp.int32, (thermal_ref.shape[0], CZ), 1) < CZ // 2
    for lon in range(2):
        field = thermal_ref[:, lon, :]
        for sums in (one_ref, two_ref):
            forced = field + warming_ref[...] * sums[2 + lon : 3 + lon, :]
            low = jnp.dot(inverse_ref[0], forced, precision=HIGHEST, preferred_element_type=F32)
            high = jnp.dot(inverse_ref[1], forced, precision=HIGHEST, preferred_element_type=F32)
            field = jnp.where(low_band, low, high)
        out_ref[:, lon, :] = field


def shifted(value, axis, by):
    count = lax.axis_size(axis)
    return lax.ppermute(value, axis, [(i, (i + by) % count) for i in range(count)])


def halos(faces):
    y_low, y_high, x_low, x_high = faces
    return (
        shifted(y_high, "grp", 1),
        shifted(y_low, "grp", -1),
        shifted(x_high, "blk", 1),
        shifted(x_low, "blk", -1),
    )


def body(
    mass_per_volume,
    flow_vector,
    magnetic_vector,
    thermal_push,
    gradient_clipping_flags,
    tracer_launch_volume,
    tracer_holder_tile,
    holder_local_offset,
    neutral_thermal_field,
    electric_voltage,
    reciprocal_operators,
    warming_by_height,
    pedersen_by_height,
):
    group = lax.axis_index("grp")
    lines = tracer_launch_volume.shape[0]
    sources = tracer_launch_volume[:, 0]
    columns = holder_local_offset[:, 0]
    zero = jnp.zeros_like(sources)
    line_rows = jnp.stack(
        [
            sources // CZ,
            sources % CZ,
            columns // CZ,
            columns % CZ,
            tracer_holder_tile[:, 0],
            zero + 1,
            zero,
            zero,
        ],
        axis=0,
    ).astype(F32)
    quarter = LATS // 4

    packed = kernel_call(
        pack_kernel,
        [shape(8, CX, CY, CZ), shape(CX, CY, CZ)] + face_shapes(8) + [shape(CX, CZ)] * 4,
        1.0,
    )(mass_per_volume, flow_vector, magnetic_vector, thermal_push, gradient_clipping_flags)
    fluid, limiter = packed[:2]
    faces, field_faces, limit_faces = packed[2:6], packed[6:10], packed[10:14]
    field_halos = halos(field_faces)
    all_halos = halos(faces)
    limit_halos = halos(limit_faces)

    slots = kernel_call(slot_kernel, shape(8, SLOTS), 1.0)(tracer_holder_tile, line_rows)
    base = kernel_call(
        base_kernel, shape(8, LATS), 2.0, [pltpu.VMEM((2 * BANDS, 50), F32)]
    )(
        reciprocal_operators,
        pedersen_by_height[:, None],
        warming_by_height[None, :],
        neutral_thermal_field,
    )

    rows_scratch = pltpu.VMEM((8, SLOTS), F32)
    stack_scratch = pltpu.VMEM((16, SLOTS), F32)
    parts_scratch = pltpu.VMEM((4 * CZ, SLOTS), BF16)

    def payload(w, near):
        return kernel_call(
            payload_kernel,
            shape(BLOCKS, 4, CZ),
            2.0,
            [pltpu.VMEM((CX * CY, 2 * CZ), F32), rows_scratch],
        )(w, *near, slots)

    def exchange(blocks):
        return lax.all_to_all(blocks, "blk", split_axis=0, concat_axis=0, tiled=True)

    def ionosphere(at, sums, potential, base_now, column):
        terms = [sums] + [shifted(sums, "grp", k) for k in range(1, 4)]
        here = kernel_call(
            functools.partial(gather_kernel, at), shape(8, LATS), 0.3
        )(*terms, potential, base_now)
        around = [shifted(here, "blk", k) for k in (2, 1)]
        around += [here]
        around += [shifted(here, "blk", k) for k in (-1, -2)]
        voltage, reply, base_next = kernel_call(
            sweep_kernel,
            [shape(2, LATS), shape(BLOCKS, 4, CZ), shape(8, LATS)],
            2.0,
            [pltpu.VMEM((4, 16, LATS), F32), pltpu.VMEM((16, LATS), F32)],
        )(*around, base_now, column)
        return here, voltage, exchange(reply), base_next

    arrived = exchange(payload(fluid, field_halos))
    middle = substep("all", False, (fluid, limiter, *all_halos, *limit_halos))
    sums, column = kernel_call(
        deposit_first_kernel,
        [shape(4, LATS), shape(8, SLOTS)],
        1.5,
        [rows_scratch, stack_scratch],
    )(arrived)
    here_one, voltage, returned, base_next = ionosphere(
        0, sums, electric_voltage, base, column
    )
    ended = substep("late", False, (middle[0], limiter, *halos(middle[1:5]), *limit_halos))
    fluid = ended[0]
    late_halos = halos(ended[1:5])
    arrived = exchange(payload(fluid, halos(ended[5:9])))
    dragged = kernel_call(
        drag_kernel,
        [shape(CX, CY, CZ)] + [shape(2, CX, CZ)] * 4,
        2.0,
        [rows_scratch, parts_scratch],
    )(returned, slots, fluid)
    speed, speed_halos = dragged[0], halos(dragged[1:5])
    sums = kernel_call(
        deposit_next_kernel, shape(4, LATS), 1.5, [rows_scratch, stack_scratch]
    )(arrived, column)
    here_two, voltage, returned, base_next = ionosphere(2, sums, voltage, base_next, column)
    middle = substep(
        "all", True, (fluid, limiter, *late_halos, *limit_halos, speed, *speed_halos)
    )
    push = kernel_call(
        scatter_kernel, shape(2, CX, CY, CZ), 2.0, [rows_scratch, parts_scratch]
    )(returned, slots)
    (conserved_quantities,) = substep(
        "final", False, (middle[0], limiter, *halos(middle[1:5]), *limit_halos, push)
    )

    start = group * quarter
    ending_thermal_state = kernel_call(
        thermal_kernel, shape(50, 2, quarter), 2.0
    )(
        lax.dynamic_slice_in_dim(neutral_thermal_field, start, quarter, 2),
        lax.dynamic_slice_in_dim(reciprocal_operators, group * 2, 2, 0),
        warming_by_height[:, None],
        lax.dynamic_slice_in_dim(here_one, start, quarter, 1),
        lax.dynamic_slice_in_dim(here_two, start, quarter, 1),
    )
    ending_electric_voltage = lax.dynamic_slice_in_dim(voltage, start, quarter, 1)
    return (conserved_quantities, ending_thermal_state, ending_electric_voltage)


def solution(mesh):
    in_specs = (
        P("blk", "grp", None),
        P(None, "blk", "grp", None),
        P(None, "blk", "grp", None),
        P("blk", "grp", None),
        P("blk", "grp", None),
        P(("grp", "blk"), None),
        P(("grp", "blk"), None),
        P(("grp", "blk"), None),
        P(None, "blk", None),
        P("blk", None),
        P(),
        P(),
        P(),
    )
    out_specs = (P(None, "blk", "grp", None), P(None, "blk", "grp"), P("blk", "grp"))
    return jax.shard_map(body, mesh=mesh, in_specs=in_specs, out_specs=out_specs, check_vma=False)
```

```python
import functools

import jax
import jax.numpy as jnp
from jax import lax
from jax.experimental import pallas as pl
from jax.experimental.pallas import tpu as pltpu
from jax.sharding import PartitionSpec as P

SWEEPS = 4
HEAT_RATIO = 5.0 / 3.0
TIME_STEP = 0.02
DRAG_RATE = 0.5
CX = 16
CY = 16
CZ = 128
BLOCKS = 32
CAP = 32
SLOTS = BLOCKS * CAP
LATS = 512
BANDS = 8
F32 = jnp.float32
BF16 = jnp.bfloat16
HIGHEST = lax.Precision.HIGHEST
VMEM_LIMIT = 40 * 1024 * 1024


def shape(*dims):
    return jax.ShapeDtypeStruct(dims, F32)


def kernel_call(body, outs, microseconds, scratch=()):
    return pl.pallas_call(
        body,
        out_shape=outs,
        scratch_shapes=list(scratch),
        compiler_params=pltpu.CompilerParams(vmem_limit_bytes=VMEM_LIMIT),
        cost_estimate=pl.CostEstimate(
            flops=0, bytes_accessed=int(microseconds * 3.3e6), transcendentals=0
        ),
    )


def half_slope(before, centre, after, half_limiter):
    forward = after - centre
    backward = centre - before
    low = jnp.minimum(backward, 0.0)
    high = jnp.maximum(backward, 0.0)
    return half_limiter * jnp.minimum(jnp.maximum(forward, low), high)


def side(w, d):
    rho, ux, uy, uz, bx, by, bz, p = w
    u = (ux, uy, uz)
    b = (bx, by, bz)
    e, f = [k for k in range(3) if k != d]
    inverse = 1.0 / rho
    m = [rho * c for c in u]
    across = b[e] * b[e] + b[f] * b[f]
    square = across + b[d] * b[d]
    kinetic = m[0] * ux + m[1] * uy + m[2] * uz
    total = p + 0.5 * square
    energy = 1.5 * p + 0.5 * (kinetic + square)
    along = ux * bx + uy * by + uz * bz
    flux = [None] * 8
    flux[0] = m[d]
    for k in range(3):
        flux[1 + k] = m[k] * u[d] - b[d] * b[k]
        if k != d:
            flux[4 + k] = u[d] * b[k] - b[d] * u[k]
    flux[1 + d] = flux[1 + d] + total
    flux[7] = (energy + total) * u[d] - b[d] * along
    sound = (HEAT_RATIO * p) * inverse
    alfven = square * inverse
    transverse = across * inverse
    gap = sound - alfven
    fast = 0.5 * (sound + alfven + jnp.sqrt(gap * gap + 4.0 * sound * transverse))
    speed = jnp.abs(u[d]) + jnp.sqrt(fast)
    return flux, [rho, m[0], m[1], m[2], bx, by, bz, energy], speed


def face_flux(left, right, d):
    flux_l, state_l, speed_l = side(left, d)
    flux_r, state_r, speed_r = side(right, d)
    speed = jnp.maximum(speed_l, speed_r)
    out = []
    for k in range(8):
        jump = speed * (state_r[k] - state_l[k])
        if flux_l[k] is None:
            out.append(-jump)
        else:
            out.append(flux_l[k] + flux_r[k] - jump)
    return out


def core():
    return lax.rem(lax.axis_index("blk"), 2)


def substep_kernel(mode, split, refs):
    refs = list(refs)
    w_ref, lim_ref = refs[:2]
    faces = refs[2:6]
    lims = refs[6:10]
    refs = refs[10:]
    if split:
        uy_ref = refs[0]
        uy_faces = refs[1:5]
        refs = refs[5:]
    if mode == "final":
        out_ref = refs[0]
        outs = ()
        refs = refs[1:]
    else:
        out_ref = refs[0]
        outs = refs[1:5]
        refs = refs[5:]
    ext, lim_ext, turned, lim_turned, across, lx, hx = refs
    even = core() == 0
    place_a = jnp.where(even, CX + 2, 0)
    place_b = CX + 2 - place_a

    def halo(which, f, r):
        if split:
            if f == 2:
                return uy_faces[which][r]
            f = f if f < 2 else f - 1
        return faces[which][2 * f + r]

    for f in range(8):
        for r in range(2):
            ext[f, place_a + r] = halo(2, f, r)
            ext[f, place_b + r] = halo(3, f, r)
            turned[f, r] = halo(0, f, r)
            turned[f, CY + 2 + r] = halo(1, f, r)
        centre = uy_ref if split and f == 2 else w_ref.at[f]
        ext[f, 2 : 2 + CX] = centre[...]
        for y in range(CY):
            turned[f, 2 + y] = centre[:, y, :]
    lim_ext[1 : 1 + CX] = 0.5 * lim_ref[...]
    place = jnp.where(even, CX + 1, 0)
    lim_ext[place] = 0.5 * lims[2][16]
    lim_ext[CX + 1 - place] = 0.5 * lims[3][16]
    lim_turned[0] = 0.5 * lims[0][16]
    lim_turned[CY + 1] = 0.5 * lims[1][16]
    for y in range(CY):
        lim_turned[1 + y] = 0.5 * lim_ref[:, y, :]

    def lowest(w, lim, d):
        left = []
        right = []
        for f in range(8):
            p, q, r, s = w[f, 0], w[f, 1], w[f, 2], w[f, 3]
            left.append(q + half_slope(p, q, r, lim[0]))
            slope = half_slope(q, r, s, lim[1])
            right.append(r - slope)
            lx[f] = r + slope
        for f, value in enumerate(face_flux(left, right, d)):
            hx[f] = value

    def next_face(w, lim, i, d):
        left = [lx[f] for f in range(8)]
        right = []
        for f in range(8):
            after = w[f, i + 3]
            slope = half_slope(w[f, i + 2], after, w[f, i + 4], lim[i + 2])
            right.append(after - slope)
            lx[f] = after + slope
        flux = face_flux(left, right, d)
        difference = []
        for f in range(8):
            difference.append(flux[f] - hx[f])
            hx[f] = flux[f]
        return difference

    lowest(turned, lim_turned, 1)

    def row(i, carry):
        for f, value in enumerate(next_face(turned, lim_turned, i, 1)):
            turned[f, i] = value
        return carry

    lax.fori_loop(0, CY, row, 0, unroll=2)
    for f in range(8):
        for x in range(CX):
            across[f, x] = turned[f, 0:CY, x, :]

    lowest(ext, lim_ext, 0)

    def plane(i, carry):
        lim = lim_ext[i + 1]
        w = [ext[f, i + 2] for f in range(8)]
        total = next_face(ext, lim_ext, i, 0)
        left = []
        right = []
        for f in range(8):
            s = half_slope(pltpu.roll(w[f], 1, 1), w[f], pltpu.roll(w[f], CZ - 1, 1), lim)
            left.append(w[f] + s)
            right.append(pltpu.roll(w[f] - s, CZ - 1, 1))
        flux = face_flux(left, right, 2)
        for f in range(8):
            total[f] = (total[f] + across[f, i]) + (flux[f] - pltpu.roll(flux[f], 1, 1))
        rho, ux, uy, uz, bx, by, bz, p = w
        m = [rho * ux, rho * uy, rho * uz]
        energy = 1.5 * p + 0.5 * (
            m[0] * ux + m[1] * uy + m[2] * uz + bx * bx + by * by + bz * bz
        )
        state = [rho, m[0], m[1], m[2], bx, by, bz, energy]
        state = [state[f] - (0.5 * TIME_STEP) * total[f] for f in range(8)]
        rho, mx, my, mz, bx, by, bz, energy = state
        if mode == "final":
            result = state
        else:
            inverse = 1.0 / rho
            p = (HEAT_RATIO - 1.0) * (
                energy
                - 0.5 * (mx * mx + my * my + mz * mz) * inverse
                - 0.5 * (bx * bx + by * by + bz * bz)
            )
            result = [rho, mx * inverse, my * inverse, mz * inverse, bx, by, bz, p]
        for f in range(8):
            out_ref[f, i] = result[f]
        return carry

    lax.fori_loop(0, CX, plane, 0, unroll=2)
    if mode != "final":
        write_faces(out_ref, outs, mode == "late")


def face_start():
    return jnp.where(core() == 0, CX - 2, 0)


def write_faces(w_ref, outs, late):
    y_low, y_high, x_a, x_b = outs
    start = face_start()
    fields = [f for f in range(8) if not (late and f == 2)]
    for g, f in enumerate(fields):
        for r in range(2):
            y_low[2 * g + r] = w_ref[f, :, r, :]
            y_high[2 * g + r] = w_ref[f, :, CY - 2 + r, :]
            x_a[2 * g + r] = w_ref[f, start + r]
            x_b[2 * g + r] = w_ref[f, CX - 2 - start + r]


def pack_kernel(rho, u, b, p, flags, w_ref, lim_ref, y_low, y_high, x_a, x_b, raw, sems):
    copies = [
        pltpu.make_async_copy(rho, w_ref.at[0], sems.at[0]),
        pltpu.make_async_copy(u, w_ref.at[1:4], sems.at[1]),
        pltpu.make_async_copy(b, w_ref.at[4:7], sems.at[2]),
        pltpu.make_async_copy(p, w_ref.at[7], sems.at[3]),
        pltpu.make_async_copy(flags, raw, sems.at[4]),
    ]
    for copy in copies:
        copy.start()
    for copy in copies:
        copy.wait()
    lim_ref[...] = raw[...].astype(F32)
    write_faces(w_ref, (y_low, y_high, x_a, x_b), False)
    start = jnp.where(core() == 0, CX - 1, 0)
    y_low[16] = lim_ref[:, 0, :]
    y_high[16] = lim_ref[:, CY - 1, :]
    x_a[16] = lim_ref[start]
    x_b[16] = lim_ref[CX - 1 - start]


def substep(mode, split, args):
    scratch = [
        pltpu.VMEM((8, CX + 4, CY, CZ), F32),
        pltpu.VMEM((CX + 2, CY, CZ), F32),
        pltpu.VMEM((8, CY + 4, CX, CZ), F32),
        pltpu.VMEM((CY + 2, CX, CZ), F32),
        pltpu.VMEM((8, CX, CY, CZ), F32),
        pltpu.VMEM((8, CY, CZ), F32),
        pltpu.VMEM((8, CY, CZ), F32),
    ]
    outs = [shape(8, CX, CY, CZ)]
    if mode == "all":
        outs += [shape(16, CX, CZ)] * 4
    elif mode == "late":
        outs += [shape(14, CX, CZ)] * 4

    def body(*refs):
        substep_kernel(mode, split, refs)

    return kernel_call(body, outs, 5.0, scratch)(*args)


def rounded_parts(value, count):
    parts = []
    for _ in range(count):
        part = value.astype(BF16).astype(F32)
        parts.append(part)
        value = value - part
    return parts


def one_hot(positions, extent):
    rows = lax.broadcasted_iota(jnp.int32, (extent, SLOTS), 0)
    return rows == positions.astype(jnp.int32)


def spread(rows, out_ref, first):
    for t in range(SLOTS // CZ):
        tile = rows[:, t * CZ : (t + 1) * CZ]
        for j in range(CZ // CAP):
            moved = tile if j == 0 else pltpu.roll(tile, CZ - CAP * j, 1)
            out_ref[t * (CZ // CAP) + j, first : first + 4, :] = moved[0:4]


def collect(block_ref, rows_ref, first):
    lane = lax.broadcasted_iota(jnp.int32, (8, CZ), 1) // CAP
    per = CZ // CAP
    for t in range(SLOTS // CZ):
        total = jnp.zeros((8, CZ), F32)
        for j in range(per):
            block = block_ref[t * per + j, first : first + 4, :]
            block = jnp.concatenate([block, block], axis=0)
            moved = block if j == 0 else pltpu.roll(block, CAP * j, 1)
            total = jnp.where(lane == j, moved, total)
        rows_ref[:, t * CZ : (t + 1) * CZ] = total


def slot_kernel(owner_ref, rows_ref, out_ref):
    count = owner_ref.shape[0]
    owner = owner_ref[...]
    others = rows_ref[4:5, :].astype(jnp.int32)
    here = lax.broadcasted_iota(jnp.int32, (count, count), 0)
    there = lax.broadcasted_iota(jnp.int32, (count, count), 1)
    earlier = jnp.where((owner == others) & (there < here), 1.0, 0.0)
    rank = jnp.sum(earlier, axis=1, keepdims=True)
    slot = owner * CAP + rank.astype(jnp.int32)
    lanes = lax.broadcasted_iota(jnp.int32, (count, SLOTS), 1)
    table = jnp.where(lanes == slot, 1.0, 0.0).astype(BF16)
    found = jnp.dot(rows_ref[...].astype(BF16), table, preferred_element_type=F32)
    out_ref[...] = found
    out_ref[0:1, :] = found[0:1] + found[5:6] - 1.0
    out_ref[2:3, :] = found[2:3] * CZ + found[3:4]


def payload_kernel(fx, fy, w_ref, y_low, y_high, x_a, x_b, slot_ref, out_ref, fields, rows):
    iota = lax.broadcasted_iota(jnp.int32, (CY, CZ), 0)
    even = core() == 0
    by_low = jnp.where(even, x_b[2 * fy + 1], x_a[2 * fy + 1])
    by_high = jnp.where(even, x_a[2 * fy], x_b[2 * fy])
    bx_low = y_low[2 * fx + 1]
    bx_high = y_high[2 * fx]
    for x in range(CX):
        east = by_high if x == CX - 1 else w_ref[5, x + 1]
        west = by_low if x == 0 else w_ref[5, x - 1]
        bx = w_ref[4, x]
        north = jnp.where(iota == CY - 1, bx_high[x : x + 1, :], pltpu.roll(bx, CY - 1, 0))
        south = jnp.where(iota == 0, bx_low[x : x + 1, :], pltpu.roll(bx, 1, 0))
        p = w_ref[7, x]
        fields[x * CY : (x + 1) * CY, 0:CZ] = 0.5 * (east - west) - 0.5 * (north - south)
        fields[x * CY : (x + 1) * CY, CZ : 2 * CZ] = p * jnp.sqrt(p / w_ref[0, x])
    cells = one_hot(slot_ref[0:1, :], CX * CY).astype(F32).astype(BF16)
    levels = one_hot(slot_ref[1:2, :], CZ)
    across = fields[...].T
    found = jnp.zeros((2 * CZ, SLOTS), F32)
    for part in rounded_parts(across, 3):
        found = found + jnp.dot(part.astype(BF16), cells, preferred_element_type=F32)
    rows[...] = slot_ref[...]
    for v in range(2):
        kept = jnp.where(levels, found[v * CZ : (v + 1) * CZ], 0.0)
        rows[v : v + 1, :] = jnp.sum(kept, axis=0, keepdims=True)
    spread(rows[...], out_ref, 0)


def deposit(rows, column, stack):
    upper = column >= float(LATS)
    place = one_hot(jnp.where(upper, column - LATS, column), LATS).astype(F32).astype(BF16)
    for v in range(2):
        for lon in range(2):
            kept = jnp.where(upper == (lon == 1), rows[v : v + 1, :], 0.0)
            for k, part in enumerate(rounded_parts(kept, 3)):
                at = 4 * k + 2 * v + lon
                stack[at : at + 1, :] = part
    stack[12:16, :] = jnp.zeros((4, SLOTS), F32)
    total = lax.dot_general(
        stack[...].astype(BF16), place, (((1,), (1,)), ((), ())), preferred_element_type=F32
    )
    return total[0:4] + total[4:8] + total[8:12]


def folded(value, out_ref, layer):
    for t in range(LATS // CZ):
        out_ref[layer, 4 * t : 4 * t + 4, :] = value[:, t * CZ : (t + 1) * CZ]


def unfolded(ref, layer):
    return [ref[layer, 4 * t : 4 * t + 4, :] for t in range(LATS // CZ)]


def deposit_first_kernel(block_ref, low_in, high_in, low_out, high_out, sums, column_ref, rows, stack):
    collect(block_ref, rows, 0)
    column_ref[...] = rows[...]
    value = deposit(rows[...], rows[2:3, :], stack)
    count = low_in.shape[0]
    low_out[0:count] = low_in[...]
    high_out[0:count] = high_in[...]
    for out_ref, layer in ((low_out, count), (high_out, count), (sums, 0)):
        folded(value, out_ref, layer)


def scatter(block_ref, first, slot_ref, rows, parts):
    collect(block_ref, rows, first)
    weight = DRAG_RATE * rows[1:2, :]
    cells = one_hot(slot_ref[0:1, :], CX * CY).astype(F32).astype(BF16)
    levels = one_hot(slot_ref[1:2, :], CZ)
    for v, value in enumerate((weight * rows[0:1, :], weight)):
        for k, part in enumerate(rounded_parts(value, 2)):
            at = (2 * v + k) * CZ
            parts[at : at + CZ, :] = jnp.where(levels, part, 0.0).astype(BF16)
    total = lax.dot_general(
        cells, parts[...], (((1,), (1,)), ((), ())), preferred_element_type=F32
    )
    first = total[:, 0:CZ] + total[:, CZ : 2 * CZ]
    second = total[:, 2 * CZ : 3 * CZ] + total[:, 3 * CZ :]
    return first.reshape(CX, CY, CZ), second.reshape(CX, CY, CZ)


def drag_kernel(
    block_ref, slot_ref, column_ref, w_ref, out_ref, y_low, y_high, x_a, x_b, sums, rows, parts, stack
):
    collect(block_ref, rows, 0)
    value = deposit(rows[...], column_ref[2:3, :], stack)
    for out_ref_, layer in ((y_low, 2), (y_high, 2), (sums, 0)):
        folded(value, out_ref_, layer)
    first, second = scatter(block_ref, 4, slot_ref, rows, parts)
    out_ref[...] = w_ref[2] * (1.0 - second) + first
    start = face_start()
    for r in range(2):
        y_low[r] = out_ref[:, r, :]
        y_high[r] = out_ref[:, CY - 2 + r, :]
        x_a[r] = out_ref[start + r]
        x_b[r] = out_ref[CX - 2 - start + r]


def last_drag_kernel(block_ref, slot_ref, u_ref, out_ref, rows, parts):
    first, second = scatter(block_ref, 0, slot_ref, rows, parts)
    out_ref[...] = u_ref[...]
    rho = u_ref[0]
    my = u_ref[2]
    added = rho * first - my * second
    out_ref[2] = my + added
    out_ref[7] = u_ref[7] + (my * added + 0.5 * added * added) / rho


def base_kernel(inverse_ref, pedersen_ref, warming_ref, thermal_ref, out_ref, factors):
    levels = pedersen_ref.shape[0]
    for band in range(BANDS):
        factors[band : band + 1, :] = jnp.sum(
            pedersen_ref[...] * inverse_ref[band], axis=0, keepdims=True
        )
    once = factors[0:BANDS, :]
    for band in range(BANDS):
        twice = jnp.dot(once, inverse_ref[band], precision=HIGHEST, preferred_element_type=F32)
        factors[BANDS + band : BANDS + band + 1, :] = twice[band : band + 1, :]
    both = factors[...]
    lane_band = lax.broadcasted_iota(jnp.int32, (BANDS, LATS), 1) // (LATS // BANDS)
    own = lane_band == lax.broadcasted_iota(jnp.int32, (BANDS, LATS), 0)

    def pick(values):
        return jnp.sum(jnp.where(own, values, 0.0), axis=0, keepdims=True)

    for lon in range(2):
        field = thermal_ref[:, lon, :]
        found = jnp.dot(both, field, precision=HIGHEST, preferred_element_type=F32)
        out_ref[lon : lon + 1, :] = pick(found[0:BANDS])
        out_ref[2 + lon : 3 + lon, :] = pick(found[BANDS:])
    response = jnp.sum(both * warming_ref[...], axis=1, keepdims=True)
    out_ref[4:5, :] = pick(jnp.broadcast_to(response[0:BANDS], (BANDS, LATS)))
    out_ref[5:6, :] = pick(jnp.broadcast_to(response[BANDS:], (BANDS, LATS)))
    out_ref[6:8, :] = jnp.zeros((2, LATS), F32)


def gather_kernel(
    at, own, low, high, far, potential, base, a_in, b_in, a_out, b_out, here_ref
):
    count = a_in.shape[0]
    a_out[0:count] = a_in[...]
    b_out[0:count] = b_in[...]
    parts = [
        unfolded(own, 0),
        unfolded(low, low.shape[0] - 1),
        unfolded(high, high.shape[0] - 1),
        unfolded(far, 0),
    ]
    for t in range(LATS // CZ):
        lanes = slice(t * CZ, (t + 1) * CZ)
        total = (parts[0][t] + parts[1][t]) + (parts[2][t] + parts[3][t])
        row = (t % 2) * 8
        for out_ref, layer in ((a_out, count), (b_out, count), (here_ref, 0)):
            out_ref[layer + t // 2, row : row + 4, :] = total
            out_ref[layer + t // 2, row + 4 : row + 6, :] = potential[:, lanes]
            out_ref[layer + t // 2, row + 6 : row + 8, :] = base[at : at + 2, lanes]


def flat(ref, first):
    pieces = [ref[first + t // 2, (t % 2) * 8 : (t % 2) * 8 + 8, :] for t in range(LATS // CZ)]
    return jnp.concatenate(pieces, axis=1)


def sweep_kernel(m2, x_a, here_ref, x_b, p2, base, column_ref, *refs):
    payload = refs[0] if len(refs) == 7 else None
    out_v, out_block, out_base, out_here, ext, table = refs[-6:]
    even = core() == 0
    mate = flat(x_a, x_a.shape[0] - 2)
    other = flat(x_b, x_b.shape[0] - 2)
    own = flat(here_ref, 0)
    out_here[...] = own
    around = (
        flat(m2, 0),
        jnp.where(even, other, mate),
        own,
        jnp.where(even, mate, other),
        flat(p2, 0),
    )
    for at, value in enumerate(around):
        for k in range(4):
            ext[k, 2 * at : 2 * at + 2, :] = value[2 * k : 2 * k + 2, :]
    for k in range(4):
        ext[k, 10:16, :] = jnp.ones((6, LATS), F32)
    source = ext[0]
    heat = ext[1]
    potential = ext[2]
    conductance = ext[3] + base[4:5, :] * heat
    lane = lax.broadcasted_iota(jnp.int32, (16, LATS), 1)
    first = lane == 0
    last = lane == LATS - 1

    def up(v):
        return jnp.where(last, 0.0, pltpu.roll(v, LATS - 1, 1))

    def down(v):
        return jnp.where(first, 0.0, pltpu.roll(v, 1, 1))

    east = 0.5 * (conductance + pltpu.roll(conductance, 15, 0))
    west = 0.5 * (conductance + pltpu.roll(conductance, 1, 0))
    north = 0.5 * (conductance + up(conductance))
    south = 0.5 * (conductance + down(conductance))
    inverse = 1.0 / (east + west + north + south)
    for _ in range(SWEEPS):
        potential = (
            east * pltpu.roll(potential, 15, 0)
            + west * pltpu.roll(potential, 1, 0)
            + north * up(potential)
            + south * down(potential)
            - source
        ) * inverse
    ext[2] = potential
    ext[3] = conductance
    out_v[...] = ext[2, 4:6, :]
    out_base[...] = base[...]
    out_base[2:4, :] = base[2:4, :] + base[5:6, :] * own[2:4, :]
    for v in range(2):
        for k, part in enumerate(rounded_parts(ext[2 + v, 4:6, :], 3)):
            table[4 * k + 2 * v : 4 * k + 2 * v + 2, :] = part
    table[12:16, :] = jnp.zeros((4, LATS), F32)
    column = column_ref[2:3, :]
    upper = column >= float(LATS)
    place = one_hot(jnp.where(upper, column - LATS, column), LATS).astype(F32).astype(BF16)
    found = jnp.dot(table[...].astype(BF16), place, preferred_element_type=F32)
    found = found[0:4] + found[4:8] + found[8:12]
    voltage = jnp.where(upper, found[1:2], found[0:1])
    weight = jnp.where(upper, found[3:4], found[2:3])
    sub = lax.broadcasted_iota(jnp.int32, (8, SLOTS), 0)
    spread(jnp.where(sub % 4 == 0, voltage, weight), out_block, 4 if payload is not None else 0)
    if payload is not None:
        for owner in range(BLOCKS):
            out_block[owner, 0:4, :] = payload[owner]


def thermal_kernel(thermal_ref, inverse_ref, warming_ref, one_ref, two_ref, out_ref):
    low_band = lax.broadcasted_iota(jnp.int32, (thermal_ref.shape[0], CZ), 1) < CZ // 2
    for lon in range(2):
        field = thermal_ref[:, lon, :]
        for sums in (one_ref, two_ref):
            forced = field + warming_ref[...] * sums[2 + lon : 3 + lon, :]
            low = jnp.dot(inverse_ref[0], forced, precision=HIGHEST, preferred_element_type=F32)
            high = jnp.dot(inverse_ref[1], forced, precision=HIGHEST, preferred_element_type=F32)
            field = jnp.where(low_band, low, high)
        out_ref[:, lon, :] = field


def shifted(value, axis, by):
    count = lax.axis_size(axis)
    return lax.ppermute(value, axis, [(i, (i + by) % count) for i in range(count)])


def swapped(value, first):
    count = lax.axis_size("blk")
    pairs = [(i, (i + 1) % count) for i in range(first, count, 2)]
    return lax.ppermute(value, "blk", pairs + [(j, i) for i, j in pairs])


def halos(faces):
    y_low, y_high, x_a, x_b = faces
    return (
        shifted(y_high, "grp", 1),
        shifted(y_low, "grp", -1),
        swapped(x_a, 0),
        swapped(x_b, 1),
    )


def body(
    mass_per_volume,
    flow_vector,
    magnetic_vector,
    thermal_push,
    gradient_clipping_flags,
    tracer_launch_volume,
    tracer_holder_tile,
    holder_local_offset,
    neutral_thermal_field,
    electric_voltage,
    reciprocal_operators,
    warming_by_height,
    pedersen_by_height,
):
    group = lax.axis_index("grp")
    lines = tracer_launch_volume.shape[0]
    sources = tracer_launch_volume[:, 0]
    columns = holder_local_offset[:, 0]
    zero = jnp.zeros_like(sources)
    line_rows = jnp.stack(
        [
            sources // CZ,
            sources % CZ,
            columns // CZ,
            columns % CZ,
            tracer_holder_tile[:, 0],
            zero + 1,
            zero,
            zero,
        ],
        axis=0,
    ).astype(F32)
    quarter = LATS // 4

    fluid, limiter, *faces = pl.pallas_call(
        pack_kernel,
        out_shape=[shape(8, CX, CY, CZ), shape(CX, CY, CZ)] + [shape(17, CX, CZ)] * 4,
        in_specs=[pl.BlockSpec(memory_space=pltpu.HBM)] * 5,
        scratch_shapes=[pltpu.VMEM((CX, CY, CZ), jnp.int32), pltpu.SemaphoreType.DMA((5,))],
        compiler_params=pltpu.CompilerParams(vmem_limit_bytes=60 * 1024 * 1024),
    )(mass_per_volume, flow_vector, magnetic_vector, thermal_push, gradient_clipping_flags)
    first_halos = halos(faces)

    slots = kernel_call(slot_kernel, shape(8, SLOTS), 1.0)(tracer_holder_tile, line_rows)
    base = kernel_call(
        base_kernel, shape(8, LATS), 2.0, [pltpu.VMEM((2 * BANDS, 50), F32)]
    )(
        reciprocal_operators,
        pedersen_by_height[:, None],
        warming_by_height[None, :],
        neutral_thermal_field,
    )

    rows_scratch = pltpu.VMEM((8, SLOTS), F32)
    stack_scratch = pltpu.VMEM((16, SLOTS), F32)
    parts_scratch = pltpu.VMEM((4 * CZ, SLOTS), BF16)

    def payload(w, near, fx, fy):
        return kernel_call(
            functools.partial(payload_kernel, fx, fy),
            shape(BLOCKS, 4, CZ),
            2.0,
            [pltpu.VMEM((CX * CY, 2 * CZ), F32), rows_scratch],
        )(w, *near, slots)

    def exchange(blocks):
        return lax.all_to_all(blocks, "blk", split_axis=0, concat_axis=0, tiled=True)

    def gathered(at, sums, near, far, potential, base_now, x_a, x_b):
        count = x_a.shape[0] + 2
        return kernel_call(
            functools.partial(gather_kernel, at),
            [shape(count, CX, CZ)] * 2 + [shape(2, CX, CZ)],
            0.5,
        )(sums, near[0], near[1], far, potential, base_now, x_a, x_b)

    def swept(m2, x_a, here, x_b, p2, base_now, column, *payload):
        rows = 8 if payload else 4
        return kernel_call(
            sweep_kernel,
            [shape(2, LATS), shape(BLOCKS, rows, CZ), shape(8, LATS), shape(8, LATS)],
            2.0,
            [pltpu.VMEM((4, 16, LATS), F32), pltpu.VMEM((16, LATS), F32)],
        )(m2, x_a, here, x_b, p2, base_now, column, *payload)

    arrived = exchange(payload(fluid, first_halos, 4, 5))
    fluid, y_low, y_high, x_a, x_b = substep(
        "all", False, (fluid, limiter, *first_halos, *first_halos)
    )
    y_low, y_high, sums, column = kernel_call(
        deposit_first_kernel,
        [shape(17, CX, CZ)] * 2 + [shape(1, CX, CZ), shape(8, SLOTS)],
        1.5,
        [rows_scratch, stack_scratch],
    )(arrived, y_low, y_high)
    near = halos((y_low, y_high, x_a, x_b))
    far = shifted(sums, "grp", 2)
    fluid, y_low, y_high, x_a, x_b = substep(
        "late", False, (fluid, limiter, *near, *first_halos)
    )
    x_a, x_b, here = gathered(0, sums, near, far, electric_voltage, base, x_a, x_b)
    late_halos = halos((y_low, y_high, x_a, x_b))
    m2, p2 = shifted(here, "blk", 2), shifted(here, "blk", -2)
    lines = payload(fluid, late_halos, 3, 4)
    voltage, blocks, base_next, here_one = swept(
        m2, late_halos[2], here, late_halos[3], p2, base, column, lines
    )
    arrived = exchange(blocks)
    speed, *faces, sums = kernel_call(
        drag_kernel,
        [shape(CX, CY, CZ)]
        + [shape(3, CX, CZ)] * 2
        + [shape(2, CX, CZ)] * 2
        + [shape(1, CX, CZ)],
        2.0,
        [rows_scratch, parts_scratch, stack_scratch],
    )(arrived, slots, column, fluid)
    speed_halos = halos(faces)
    far = shifted(sums, "grp", 2)
    fluid, y_low, y_high, x_a, x_b = substep(
        "all", True, (fluid, limiter, *late_halos, *first_halos, speed, *speed_halos)
    )
    x_a, x_b, here = gathered(2, sums, speed_halos, far, voltage, base_next, x_a, x_b)
    near = halos((y_low, y_high, x_a, x_b))
    m2, p2 = shifted(here, "blk", 2), shifted(here, "blk", -2)
    voltage, blocks, _, here_two = swept(m2, near[2], here, near[3], p2, base_next, column)
    returned = exchange(blocks)
    (state,) = substep("final", False, (fluid, limiter, *near, *first_halos))
    conserved_quantities = kernel_call(
        last_drag_kernel, shape(8, CX, CY, CZ), 1.5, [rows_scratch, parts_scratch]
    )(returned, slots, state)

    start = group * quarter
    ending_thermal_state = kernel_call(
        thermal_kernel, shape(50, 2, quarter), 2.0
    )(
        lax.dynamic_slice_in_dim(neutral_thermal_field, start, quarter, 2),
        lax.dynamic_slice_in_dim(reciprocal_operators, group * 2, 2, 0),
        warming_by_height[:, None],
        lax.dynamic_slice_in_dim(here_one, start, quarter, 1),
        lax.dynamic_slice_in_dim(here_two, start, quarter, 1),
    )
    ending_electric_voltage = lax.dynamic_slice_in_dim(voltage, start, quarter, 1)
    return (conserved_quantities, ending_thermal_state, ending_electric_voltage)


def solution(mesh):
    in_specs = (
        P("blk", "grp", None),
        P(None, "blk", "grp", None),
        P(None, "blk", "grp", None),
        P("blk", "grp", None),
        P("blk", "grp", None),
        P(("grp", "blk"), None),
        P(("grp", "blk"), None),
        P(("grp", "blk"), None),
        P(None, "blk", None),
        P("blk", None),
        P(),
        P(),
        P(),
    )
    out_specs = (P(None, "blk", "grp", None), P(None, "blk", "grp"), P("blk", "grp"))
    return jax.shard_map(body, mesh=mesh, in_specs=in_specs, out_specs=out_specs, check_vma=False)
```

```python
import functools

import jax
import jax.numpy as jnp
from jax import lax
from jax.experimental import pallas as pl
from jax.experimental.pallas import tpu as pltpu
from jax.sharding import PartitionSpec as P

SWEEPS = 4
HEAT_RATIO = 5.0 / 3.0
TIME_STEP = 0.02
DRAG_RATE = 0.5
CX = 16
CY = 16
CZ = 128
BLOCKS = 32
CAP = 32
SLOTS = BLOCKS * CAP
LATS = 512
BANDS = 8
F32 = jnp.float32
BF16 = jnp.bfloat16
HIGHEST = lax.Precision.HIGHEST
VMEM_LIMIT = 16 * 1024 * 1024


def shape(*dims):
    return jax.ShapeDtypeStruct(dims, F32)


def kernel_call(body, outs, microseconds, scratch=()):
    return pl.pallas_call(
        body,
        out_shape=outs,
        scratch_shapes=list(scratch),
        compiler_params=pltpu.CompilerParams(vmem_limit_bytes=VMEM_LIMIT),
        cost_estimate=pl.CostEstimate(
            flops=0, bytes_accessed=int(microseconds * 3.3e6), transcendentals=0
        ),
    )


def half_slope(before, centre, after, half_limiter):
    forward = after - centre
    backward = centre - before
    low = jnp.minimum(backward, 0.0)
    high = jnp.maximum(backward, 0.0)
    return half_limiter * jnp.minimum(jnp.maximum(forward, low), high)


def root(v):
    return v * lax.rsqrt(jnp.maximum(v, 1e-30))


def side(w, d):
    rho, ux, uy, uz, bx, by, bz, p = w
    u = (ux, uy, uz)
    b = (bx, by, bz)
    e, f = [k for k in range(3) if k != d]
    inverse = 1.0 / rho
    m = [rho * c for c in u]
    across = b[e] * b[e] + b[f] * b[f]
    square = across + b[d] * b[d]
    kinetic = m[0] * ux + m[1] * uy + m[2] * uz
    total = p + 0.5 * square
    energy = 1.5 * p + 0.5 * (kinetic + square)
    along = ux * bx + uy * by + uz * bz
    flux = [None] * 8
    flux[0] = m[d]
    for k in range(3):
        flux[1 + k] = m[k] * u[d] - b[d] * b[k]
        if k != d:
            flux[4 + k] = u[d] * b[k] - b[d] * u[k]
    flux[1 + d] = flux[1 + d] + total
    flux[7] = (energy + total) * u[d] - b[d] * along
    sound = (HEAT_RATIO * p) * inverse
    alfven = square * inverse
    transverse = across * inverse
    gap = sound - alfven
    fast = 0.5 * (sound + alfven + root(gap * gap + 4.0 * sound * transverse))
    speed = jnp.abs(u[d]) + root(fast)
    return flux, [rho, m[0], m[1], m[2], bx, by, bz, energy], speed


def face_flux(left, right, d):
    flux_l, state_l, speed_l = side(left, d)
    flux_r, state_r, speed_r = side(right, d)
    speed = jnp.maximum(speed_l, speed_r)
    out = []
    for k in range(8):
        jump = speed * (state_r[k] - state_l[k])
        if flux_l[k] is None:
            out.append(-jump)
        else:
            out.append(flux_l[k] + flux_r[k] - jump)
    return out


def core():
    return lax.rem(lax.axis_index("blk"), 2)


def substep_kernel(mode, split, refs):
    refs = list(refs)
    w_ref, lim_ref = refs[:2]
    faces = refs[2:6]
    refs = refs[6:]
    if mode == "first":
        lims = [face[16] for face in faces]
    else:
        lims = [refs[0][k] for k in range(4)]
        refs = refs[1:]
    if split:
        uy_ref = refs[0]
        uy_faces = refs[1:5]
        refs = refs[5:]
    if mode == "final":
        out_ref = refs[0]
        outs = ()
        refs = refs[1:]
    else:
        out_ref = refs[0]
        outs = refs[1:5]
        refs = refs[5:]
    if mode == "first":
        for k in range(4):
            refs[0][k] = lims[k]
        refs = refs[1:]
    ext, lim_ext, turned, lim_turned, across, lx, hx = refs
    even = core() == 0
    place_a = jnp.where(even, CX + 2, 0)
    place_b = CX + 2 - place_a

    def halo(which, f, r):
        if split:
            if f == 2:
                return uy_faces[which][r]
            f = f if f < 2 else f - 1
        return faces[which][2 * f + r]

    for f in range(8):
        for r in range(2):
            ext[f, place_a + r] = halo(2, f, r)
            ext[f, place_b + r] = halo(3, f, r)
            turned[f, r] = halo(0, f, r)
            turned[f, CY + 2 + r] = halo(1, f, r)
        centre = uy_ref if split and f == 2 else w_ref.at[f]
        ext[f, 2 : 2 + CX] = centre[...]
        for y in range(CY):
            turned[f, 2 + y] = centre[:, y, :]
    lim_ext[1 : 1 + CX] = 0.5 * lim_ref[...]
    place = jnp.where(even, CX + 1, 0)
    lim_ext[place] = 0.5 * lims[2]
    lim_ext[CX + 1 - place] = 0.5 * lims[3]
    lim_turned[0] = 0.5 * lims[0]
    lim_turned[CY + 1] = 0.5 * lims[1]
    for y in range(CY):
        lim_turned[1 + y] = 0.5 * lim_ref[:, y, :]

    def lowest(w, lim, d):
        left = []
        right = []
        for f in range(8):
            p, q, r, s = w[f, 0], w[f, 1], w[f, 2], w[f, 3]
            left.append(q + half_slope(p, q, r, lim[0]))
            slope = half_slope(q, r, s, lim[1])
            right.append(r - slope)
            lx[d, f] = r + slope
        for f, value in enumerate(face_flux(left, right, d)):
            hx[d, f] = value

    def next_face(w, lim, i, d):
        left = [lx[d, f] for f in range(8)]
        right = []
        for f in range(8):
            after = w[f, i + 3]
            slope = half_slope(w[f, i + 2], after, w[f, i + 4], lim[i + 2])
            right.append(after - slope)
            lx[d, f] = after + slope
        flux = face_flux(left, right, d)
        difference = []
        for f in range(8):
            difference.append(flux[f] - hx[d, f])
            hx[d, f] = flux[f]
        return difference

    lowest(turned, lim_turned, 1)
    lowest(ext, lim_ext, 0)

    def plane(i, carry):
        lim = lim_ext[i + 1]
        w = [ext[f, i + 2] for f in range(8)]
        total = next_face(ext, lim_ext, i, 0)
        for f, value in enumerate(next_face(turned, lim_turned, i, 1)):
            turned[f, i] = value
        left = []
        right = []
        for f in range(8):
            s = half_slope(pltpu.roll(w[f], 1, 1), w[f], pltpu.roll(w[f], CZ - 1, 1), lim)
            left.append(w[f] + s)
            right.append(pltpu.roll(w[f] - s, CZ - 1, 1))
        flux = face_flux(left, right, 2)
        for f in range(8):
            across[f, i] = total[f] + (flux[f] - pltpu.roll(flux[f], 1, 1))
        return carry

    def close(i, carry):
        w = [ext[f, i + 2] for f in range(8)]
        total = [across[f, i] for f in range(8)]
        rho, ux, uy, uz, bx, by, bz, p = w
        m = [rho * ux, rho * uy, rho * uz]
        energy = 1.5 * p + 0.5 * (
            m[0] * ux + m[1] * uy + m[2] * uz + bx * bx + by * by + bz * bz
        )
        state = [rho, m[0], m[1], m[2], bx, by, bz, energy]
        state = [state[f] - (0.5 * TIME_STEP) * total[f] for f in range(8)]
        rho, mx, my, mz, bx, by, bz, energy = state
        if mode == "final":
            result = state
        else:
            inverse = 1.0 / rho
            p = (HEAT_RATIO - 1.0) * (
                energy
                - 0.5 * (mx * mx + my * my + mz * mz) * inverse
                - 0.5 * (bx * bx + by * by + bz * bz)
            )
            result = [rho, mx * inverse, my * inverse, mz * inverse, bx, by, bz, p]
        for f in range(8):
            out_ref[f, i] = result[f]
        return carry

    lax.fori_loop(0, CX, plane, 0, unroll=2)
    for f in range(8):
        for x in range(CX):
            across[f, x] = across[f, x] + turned[f, 0:CY, x, :]
    lax.fori_loop(0, CX, close, 0, unroll=4)
    if mode != "final":
        write_faces(out_ref, outs, mode == "late")


def face_start():
    return jnp.where(core() == 0, CX - 2, 0)


def write_faces(w_ref, outs, late):
    y_low, y_high, x_a, x_b = outs
    start = face_start()
    fields = [f for f in range(8) if not (late and f == 2)]
    for g, f in enumerate(fields):
        for r in range(2):
            y_low[2 * g + r] = w_ref[f, :, r, :]
            y_high[2 * g + r] = w_ref[f, :, CY - 2 + r, :]
            x_a[2 * g + r] = w_ref[f, start + r]
            x_b[2 * g + r] = w_ref[f, CX - 2 - start + r]


def pack_kernel(rho, u, b, p, flags, w_ref, lim_ref, y_low, y_high, x_a, x_b, raw, sems):
    copies = [
        pltpu.make_async_copy(rho, w_ref.at[0], sems.at[0]),
        pltpu.make_async_copy(u, w_ref.at[1:4], sems.at[1]),
        pltpu.make_async_copy(b, w_ref.at[4:7], sems.at[2]),
        pltpu.make_async_copy(p, w_ref.at[7], sems.at[3]),
        pltpu.make_async_copy(flags, raw, sems.at[4]),
    ]
    for copy in copies:
        copy.start()
    for copy in copies:
        copy.wait()
    lim_ref[...] = raw[...].astype(F32)
    write_faces(w_ref, (y_low, y_high, x_a, x_b), False)
    start = jnp.where(core() == 0, CX - 1, 0)
    y_low[16] = lim_ref[:, 0, :]
    y_high[16] = lim_ref[:, CY - 1, :]
    x_a[16] = lim_ref[start]
    x_b[16] = lim_ref[CX - 1 - start]


def substep(mode, split, args):
    scratch = [
        pltpu.VMEM((8, CX + 4, CY, CZ), F32),
        pltpu.VMEM((CX + 2, CY, CZ), F32),
        pltpu.VMEM((8, CY + 4, CX, CZ), F32),
        pltpu.VMEM((CY + 2, CX, CZ), F32),
        pltpu.VMEM((8, CX, CY, CZ), F32),
        pltpu.VMEM((2, 8, CY, CZ), F32),
        pltpu.VMEM((2, 8, CY, CZ), F32),
    ]
    outs = [shape(8, CX, CY, CZ)]
    if mode in ("first", "all"):
        outs += [shape(16, CX, CZ)] * 4
    elif mode == "late":
        outs += [shape(14, CX, CZ)] * 4
    if mode == "first":
        outs += [shape(4, CX, CZ)]

    def body(*refs):
        substep_kernel(mode, split, refs)

    return kernel_call(body, outs, 5.0, scratch)(*args)


def rounded_parts(value, count):
    parts = []
    for _ in range(count):
        part = value.astype(BF16).astype(F32)
        parts.append(part)
        value = value - part
    return parts


def one_hot(positions, extent):
    rows = lax.broadcasted_iota(jnp.int32, (extent, SLOTS), 0)
    return rows == positions.astype(jnp.int32)


def spread(rows, out_ref, first, last):
    for t in range(SLOTS // CZ):
        tile = rows[:, t * CZ : (t + 1) * CZ]
        for j in range(CZ // CAP):
            moved = tile if j == 0 else pltpu.roll(tile, CZ - CAP * j, 1)
            out_ref[t * (CZ // CAP) + j, first:last, :] = moved[first:last]


def collect(block_ref, rows_ref):
    lane = lax.broadcasted_iota(jnp.int32, (8, CZ), 1) // CAP
    per = CZ // CAP
    for t in range(SLOTS // CZ):
        total = jnp.zeros((8, CZ), F32)
        for j in range(per):
            block = block_ref[t * per + j]
            block = jnp.concatenate([block, block], axis=0)
            moved = block if j == 0 else pltpu.roll(block, CAP * j, 1)
            total = jnp.where(lane == j, moved, total)
        rows_ref[:, t * CZ : (t + 1) * CZ] = total


def slot_kernel(owner_ref, rows_ref, out_ref):
    count = owner_ref.shape[0]
    owner = owner_ref[...]
    others = rows_ref[4:5, :].astype(jnp.int32)
    here = lax.broadcasted_iota(jnp.int32, (count, count), 0)
    there = lax.broadcasted_iota(jnp.int32, (count, count), 1)
    earlier = jnp.where((owner == others) & (there < here), 1.0, 0.0)
    rank = jnp.sum(earlier, axis=1, keepdims=True)
    slot = owner * CAP + rank.astype(jnp.int32)
    lanes = lax.broadcasted_iota(jnp.int32, (count, SLOTS), 1)
    table = jnp.where(lanes == slot, 1.0, 0.0).astype(BF16)
    found = jnp.dot(rows_ref[...].astype(BF16), table, preferred_element_type=F32)
    out_ref[...] = found
    out_ref[0:1, :] = found[0:1] + found[5:6] - 1.0
    out_ref[2:3, :] = found[2:3] * CZ + found[3:4]


def payload_kernel(fx, fy, w_ref, y_low, y_high, x_a, x_b, slot_ref, out_ref, fields, rows):
    iota = lax.broadcasted_iota(jnp.int32, (CY, CZ), 0)
    even = core() == 0
    by_low = jnp.where(even, x_b[2 * fy + 1], x_a[2 * fy + 1])
    by_high = jnp.where(even, x_a[2 * fy], x_b[2 * fy])
    bx_low = y_low[2 * fx + 1]
    bx_high = y_high[2 * fx]
    for x in range(CX):
        east = by_high if x == CX - 1 else w_ref[5, x + 1]
        west = by_low if x == 0 else w_ref[5, x - 1]
        bx = w_ref[4, x]
        north = jnp.where(iota == CY - 1, bx_high[x : x + 1, :], pltpu.roll(bx, CY - 1, 0))
        south = jnp.where(iota == 0, bx_low[x : x + 1, :], pltpu.roll(bx, 1, 0))
        p = w_ref[7, x]
        fields[x * CY : (x + 1) * CY, 0:CZ] = 0.5 * (east - west) - 0.5 * (north - south)
        fields[x * CY : (x + 1) * CY, CZ : 2 * CZ] = p * jnp.sqrt(p / w_ref[0, x])
    cells = one_hot(slot_ref[0:1, :], CX * CY).astype(F32).astype(BF16)
    levels = one_hot(slot_ref[1:2, :], CZ)
    across = fields[...].T
    found = jnp.zeros((2 * CZ, SLOTS), F32)
    for part in rounded_parts(across, 3):
        found = found + jnp.dot(part.astype(BF16), cells, preferred_element_type=F32)
    rows[...] = slot_ref[...]
    for v in range(2):
        kept = jnp.where(levels, found[v * CZ : (v + 1) * CZ], 0.0)
        rows[v : v + 1, :] = jnp.sum(kept, axis=0, keepdims=True)
    spread(rows[...], out_ref, 0, 4)


def deposit(rows, column, stack):
    upper = column >= float(LATS)
    place = one_hot(jnp.where(upper, column - LATS, column), LATS).astype(F32).astype(BF16)
    for v in range(2):
        for lon in range(2):
            kept = jnp.where(upper == (lon == 1), rows[v : v + 1, :], 0.0)
            for k, part in enumerate(rounded_parts(kept, 3)):
                at = 4 * k + 2 * v + lon
                stack[at : at + 1, :] = part
    stack[12:16, :] = jnp.zeros((4, SLOTS), F32)
    total = lax.dot_general(
        stack[...].astype(BF16), place, (((1,), (1,)), ((), ())), preferred_element_type=F32
    )
    return total[0:4] + total[4:8] + total[8:12]


def folded(value, out_ref, layer):
    for t in range(LATS // CZ):
        out_ref[layer, 4 * t : 4 * t + 4, :] = value[:, t * CZ : (t + 1) * CZ]


def unfolded(ref, layer):
    return [ref[layer, 4 * t : 4 * t + 4, :] for t in range(LATS // CZ)]


def deposit_first_kernel(block_ref, low_in, high_in, low_out, high_out, sums, column_ref, rows, stack):
    collect(block_ref, rows)
    column_ref[...] = rows[...]
    value = deposit(rows[...], rows[2:3, :], stack)
    count = low_in.shape[0]
    low_out[0:count] = low_in[...]
    high_out[0:count] = high_in[...]
    for out_ref, layer in ((low_out, count), (high_out, count), (sums, 0)):
        folded(value, out_ref, layer)


def scatter(rows, at, slot_ref, parts):
    weight = DRAG_RATE * rows[at + 1 : at + 2, :]
    cells = one_hot(slot_ref[0:1, :], CX * CY).astype(F32).astype(BF16)
    levels = one_hot(slot_ref[1:2, :], CZ)
    for v, value in enumerate((weight * rows[at : at + 1, :], weight)):
        for k, part in enumerate(rounded_parts(value, 2)):
            at = (2 * v + k) * CZ
            parts[at : at + CZ, :] = jnp.where(levels, part, 0.0).astype(BF16)
    total = lax.dot_general(
        cells, parts[...], (((1,), (1,)), ((), ())), preferred_element_type=F32
    )
    first = total[:, 0:CZ] + total[:, CZ : 2 * CZ]
    second = total[:, 2 * CZ : 3 * CZ] + total[:, 3 * CZ :]
    return first.reshape(CX, CY, CZ), second.reshape(CX, CY, CZ)


def drag_kernel(
    block_ref, slot_ref, column_ref, w_ref, out_ref, y_low, y_high, x_a, x_b, sums, rows, parts, stack
):
    collect(block_ref, rows)
    value = deposit(rows[...], column_ref[2:3, :], stack)
    for out_ref_, layer in ((y_low, 2), (y_high, 2), (sums, 0)):
        folded(value, out_ref_, layer)
    first, second = scatter(rows, 2, slot_ref, parts)
    out_ref[...] = w_ref[2] * (1.0 - second) + first
    start = face_start()
    for r in range(2):
        y_low[r] = out_ref[:, r, :]
        y_high[r] = out_ref[:, CY - 2 + r, :]
        x_a[r] = out_ref[start + r]
        x_b[r] = out_ref[CX - 2 - start + r]


def last_drag_kernel(block_ref, slot_ref, u_ref, out_ref, rows, parts, changed, sems):
    kept = [
        pltpu.make_async_copy(u_ref.at[0:2], out_ref.at[0:2], sems.at[0]),
        pltpu.make_async_copy(u_ref.at[3:7], out_ref.at[3:7], sems.at[1]),
    ]
    for copy in kept:
        copy.start()
    collect(block_ref, rows)
    first, second = scatter(rows, 0, slot_ref, parts)
    rho = u_ref[0]
    my = u_ref[2]
    added = rho * first - my * second
    changed[0] = my + added
    changed[1] = u_ref[7] + (my * added + 0.5 * added * added) / rho
    new = [
        pltpu.make_async_copy(changed.at[0], out_ref.at[2], sems.at[2]),
        pltpu.make_async_copy(changed.at[1], out_ref.at[7], sems.at[3]),
    ]
    for copy in new:
        copy.start()
    for copy in kept + new:
        copy.wait()


def base_kernel(inverse_ref, pedersen_ref, warming_ref, thermal_ref, out_ref, factors):
    levels = pedersen_ref.shape[0]
    for band in range(BANDS):
        factors[band : band + 1, :] = jnp.sum(
            pedersen_ref[...] * inverse_ref[band], axis=0, keepdims=True
        )
    once = factors[0:BANDS, :]
    for band in range(BANDS):
        twice = jnp.dot(once, inverse_ref[band], precision=HIGHEST, preferred_element_type=F32)
        factors[BANDS + band : BANDS + band + 1, :] = twice[band : band + 1, :]
    both = factors[...]
    lane_band = lax.broadcasted_iota(jnp.int32, (BANDS, LATS), 1) // (LATS // BANDS)
    own = lane_band == lax.broadcasted_iota(jnp.int32, (BANDS, LATS), 0)

    def pick(values):
        return jnp.sum(jnp.where(own, values, 0.0), axis=0, keepdims=True)

    for lon in range(2):
        field = thermal_ref[:, lon, :]
        found = jnp.dot(both, field, precision=HIGHEST, preferred_element_type=F32)
        out_ref[lon : lon + 1, :] = pick(found[0:BANDS])
        out_ref[2 + lon : 3 + lon, :] = pick(found[BANDS:])
    response = jnp.sum(both * warming_ref[...], axis=1, keepdims=True)
    out_ref[4:5, :] = pick(jnp.broadcast_to(response[0:BANDS], (BANDS, LATS)))
    out_ref[5:6, :] = pick(jnp.broadcast_to(response[BANDS:], (BANDS, LATS)))
    out_ref[6:8, :] = jnp.zeros((2, LATS), F32)


def gather_kernel(
    at, own, low, high, far, potential, base, a_in, b_in, a_out, b_out, here_ref
):
    count = a_in.shape[0]
    a_out[0:count] = a_in[...]
    b_out[0:count] = b_in[...]
    parts = [
        unfolded(own, 0),
        unfolded(low, low.shape[0] - 1),
        unfolded(high, high.shape[0] - 1),
        unfolded(far, 0),
    ]
    for t in range(LATS // CZ):
        lanes = slice(t * CZ, (t + 1) * CZ)
        total = (parts[0][t] + parts[1][t]) + (parts[2][t] + parts[3][t])
        row = (t % 2) * 8
        for out_ref, layer in ((a_out, count), (b_out, count), (here_ref, 0)):
            out_ref[layer + t // 2, row : row + 4, :] = total
            out_ref[layer + t // 2, row + 4 : row + 6, :] = potential[:, lanes]
            out_ref[layer + t // 2, row + 6 : row + 8, :] = base[at : at + 2, lanes]


def flat(ref, first):
    pieces = [ref[first + t // 2, (t % 2) * 8 : (t % 2) * 8 + 8, :] for t in range(LATS // CZ)]
    return jnp.concatenate(pieces, axis=1)


def sweep_kernel(m2, x_a, here_ref, x_b, p2, base, column_ref, *refs):
    payload = refs[0] if len(refs) == 7 else None
    out_v, out_block, out_base, out_here, ext, table = refs[-6:]
    even = core() == 0
    mate = flat(x_a, x_a.shape[0] - 2)
    other = flat(x_b, x_b.shape[0] - 2)
    own = flat(here_ref, 0)
    out_here[...] = own
    around = (
        flat(m2, 0),
        jnp.where(even, other, mate),
        own,
        jnp.where(even, mate, other),
        flat(p2, 0),
    )
    for at, value in enumerate(around):
        for k in range(4):
            ext[k, 2 * at : 2 * at + 2, :] = value[2 * k : 2 * k + 2, :]
    for k in range(4):
        ext[k, 10:16, :] = jnp.ones((6, LATS), F32)
    source = ext[0]
    heat = ext[1]
    potential = ext[2]
    conductance = ext[3] + base[4:5, :] * heat
    lane = lax.broadcasted_iota(jnp.int32, (16, LATS), 1)
    first = lane == 0
    last = lane == LATS - 1

    def up(v):
        return jnp.where(last, 0.0, pltpu.roll(v, LATS - 1, 1))

    def down(v):
        return jnp.where(first, 0.0, pltpu.roll(v, 1, 1))

    east = 0.5 * (conductance + pltpu.roll(conductance, 15, 0))
    west = 0.5 * (conductance + pltpu.roll(conductance, 1, 0))
    north = 0.5 * (conductance + up(conductance))
    south = 0.5 * (conductance + down(conductance))
    inverse = 1.0 / (east + west + north + south)
    for _ in range(SWEEPS):
        potential = (
            east * pltpu.roll(potential, 15, 0)
            + west * pltpu.roll(potential, 1, 0)
            + north * up(potential)
            + south * down(potential)
            - source
        ) * inverse
    ext[2] = potential
    ext[3] = conductance
    out_v[...] = ext[2, 4:6, :]
    out_base[...] = base[...]
    out_base[2:4, :] = base[2:4, :] + base[5:6, :] * own[2:4, :]
    for v in range(2):
        for k, part in enumerate(rounded_parts(ext[2 + v, 4:6, :], 3)):
            table[4 * k + 2 * v : 4 * k + 2 * v + 2, :] = part
    table[12:16, :] = jnp.zeros((4, LATS), F32)
    column = column_ref[2:3, :]
    upper = column >= float(LATS)
    place = one_hot(jnp.where(upper, column - LATS, column), LATS).astype(F32).astype(BF16)
    found = jnp.dot(table[...].astype(BF16), place, preferred_element_type=F32)
    found = found[0:4] + found[4:8] + found[8:12]
    voltage = jnp.where(upper, found[1:2], found[0:1])
    weight = jnp.where(upper, found[3:4], found[2:3])
    sub = lax.broadcasted_iota(jnp.int32, (8, SLOTS), 0)
    rows = jnp.where(sub % 2 == 0, voltage, weight)
    if payload is None:
        spread(rows, out_block, 0, 4)
    else:
        spread(rows, out_block, 2, 4)
        for owner in range(BLOCKS):
            out_block[owner, 0:2, :] = payload[owner, 0:2, :]


def thermal_kernel(
    thermal_ref, inverse_ref, warming_ref, one_ref, two_ref, voltage_ref, out_ref, out_v, own, sem
):
    group = lax.axis_index("grp")
    lanes = pl.ds(pl.multiple_of(group * CZ, CZ), CZ)
    copy = pltpu.make_async_copy(thermal_ref.at[:, :, lanes], own, sem)
    copy.start()
    out_v[...] = voltage_ref[:, lanes]
    copy.wait()
    low_band = lax.broadcasted_iota(jnp.int32, (own.shape[0], CZ), 1) < CZ // 2
    for lon in range(2):
        field = own[:, lon, :]
        for sums in (one_ref, two_ref):
            forced = field + warming_ref[...] * sums[2 + lon : 3 + lon, lanes]
            low, high = (
                jnp.dot(
                    inverse_ref[2 * group + k],
                    forced,
                    precision=HIGHEST,
                    preferred_element_type=F32,
                )
                for k in range(2)
            )
            field = jnp.where(low_band, low, high)
        out_ref[:, lon, :] = field


def shifted(value, axis, by):
    count = lax.axis_size(axis)
    return lax.ppermute(value, axis, [(i, (i + by) % count) for i in range(count)])


def swapped(value, first):
    count = lax.axis_size("blk")
    pairs = [(i, (i + 1) % count) for i in range(first, count, 2)]
    return lax.ppermute(value, "blk", pairs + [(j, i) for i, j in pairs])


def halos(faces):
    y_low, y_high, x_a, x_b = faces
    return (
        shifted(y_high, "grp", 1),
        shifted(y_low, "grp", -1),
        swapped(x_a, 0),
        swapped(x_b, 1),
    )


def halos_and_far(faces, here):
    y_low, y_high, x_a, x_b = faces
    m2, p2 = shifted(here, "blk", 2), shifted(here, "blk", -2)
    m2, p2, x_a = lax.optimization_barrier((m2, p2, x_a))
    return halos((y_low, y_high, x_a, x_b)), m2, p2


def body(
    mass_per_volume,
    flow_vector,
    magnetic_vector,
    thermal_push,
    gradient_clipping_flags,
    tracer_launch_volume,
    tracer_holder_tile,
    holder_local_offset,
    neutral_thermal_field,
    electric_voltage,
    reciprocal_operators,
    warming_by_height,
    pedersen_by_height,
):
    sources = tracer_launch_volume[:, 0]
    columns = holder_local_offset[:, 0]
    zero = jnp.zeros_like(sources)
    line_rows = jnp.stack(
        [
            sources // CZ,
            sources % CZ,
            columns // CZ,
            columns % CZ,
            tracer_holder_tile[:, 0],
            zero + 1,
            zero,
            zero,
        ],
        axis=0,
    ).astype(F32)

    fluid, limiter, *faces = pl.pallas_call(
        pack_kernel,
        out_shape=[pltpu.VMEM((8, CX, CY, CZ), F32), pltpu.VMEM((CX, CY, CZ), F32)]
        + [pltpu.VMEM((17, CX, CZ), F32)] * 4,
        in_specs=[pl.BlockSpec(memory_space=pltpu.HBM)] * 5,
        scratch_shapes=[pltpu.VMEM((CX, CY, CZ), jnp.int32), pltpu.SemaphoreType.DMA((5,))],
        compiler_params=pltpu.CompilerParams(vmem_limit_bytes=56 * 1024 * 1024),
    )(mass_per_volume, flow_vector, magnetic_vector, thermal_push, gradient_clipping_flags)
    first_halos = halos(faces)

    slots = kernel_call(slot_kernel, shape(8, SLOTS), 1.0)(tracer_holder_tile, line_rows)
    base = kernel_call(
        base_kernel, shape(8, LATS), 2.0, [pltpu.VMEM((2 * BANDS, 50), F32)]
    )(
        reciprocal_operators,
        pedersen_by_height[:, None],
        warming_by_height[None, :],
        neutral_thermal_field,
    )

    rows_scratch = pltpu.VMEM((8, SLOTS), F32)
    stack_scratch = pltpu.VMEM((16, SLOTS), F32)
    parts_scratch = pltpu.VMEM((4 * CZ, SLOTS), BF16)

    def payload(w, near, fx, fy):
        return kernel_call(
            functools.partial(payload_kernel, fx, fy),
            shape(BLOCKS, 4, CZ),
            2.0,
            [pltpu.VMEM((CX * CY, 2 * CZ), F32), rows_scratch],
        )(w, *near, slots)

    def exchange(blocks):
        return lax.all_to_all(blocks, "blk", split_axis=0, concat_axis=0, tiled=True)

    def gathered(at, sums, near, far, potential, base_now, x_a, x_b):
        count = x_a.shape[0] + 2
        return kernel_call(
            functools.partial(gather_kernel, at),
            [shape(count, CX, CZ)] * 2 + [shape(2, CX, CZ)],
            0.5,
        )(sums, near[0], near[1], far, potential, base_now, x_a, x_b)

    def swept(m2, x_a, here, x_b, p2, base_now, column, *payload):
        return kernel_call(
            sweep_kernel,
            [shape(2, LATS), shape(BLOCKS, 4, CZ), shape(8, LATS), shape(8, LATS)],
            2.0,
            [pltpu.VMEM((4, 16, LATS), F32), pltpu.VMEM((16, LATS), F32)],
        )(m2, x_a, here, x_b, p2, base_now, column, *payload)

    arrived = exchange(payload(fluid, first_halos, 4, 5))
    fluid, y_low, y_high, x_a, x_b, limits = substep(
        "first", False, (fluid, limiter, *first_halos)
    )
    y_low, y_high, sums, column = kernel_call(
        deposit_first_kernel,
        [shape(17, CX, CZ)] * 2 + [shape(1, CX, CZ), shape(8, SLOTS)],
        1.5,
        [rows_scratch, stack_scratch],
    )(arrived, y_low, y_high)
    near = halos((y_low, y_high, x_a, x_b))
    far = shifted(sums, "grp", 2)
    fluid, y_low, y_high, x_a, x_b = substep(
        "late", False, (fluid, limiter, *near, limits)
    )
    x_a, x_b, here = gathered(0, sums, near, far, electric_voltage, base, x_a, x_b)
    late_halos, m2, p2 = halos_and_far((y_low, y_high, x_a, x_b), here)
    lines = payload(fluid, late_halos, 3, 4)
    voltage, blocks, base_next, here_one = swept(
        m2, late_halos[2], here, late_halos[3], p2, base, column, lines
    )
    arrived = exchange(blocks)
    speed, *faces, sums = kernel_call(
        drag_kernel,
        [shape(CX, CY, CZ)]
        + [shape(3, CX, CZ)] * 2
        + [shape(2, CX, CZ)] * 2
        + [shape(1, CX, CZ)],
        2.0,
        [rows_scratch, parts_scratch, stack_scratch],
    )(arrived, slots, column, fluid)
    speed_halos = halos(faces)
    far = shifted(sums, "grp", 2)
    fluid, y_low, y_high, x_a, x_b = substep(
        "all", True, (fluid, limiter, *late_halos, limits, speed, *speed_halos)
    )
    x_a, x_b, here = gathered(2, sums, speed_halos, far, voltage, base_next, x_a, x_b)
    near, m2, p2 = halos_and_far((y_low, y_high, x_a, x_b), here)
    voltage, blocks, _, here_two = swept(m2, near[2], here, near[3], p2, base_next, column)
    returned = exchange(blocks)
    (state,) = substep("final", False, (fluid, limiter, *near, limits))
    vmem = pl.BlockSpec(memory_space=pltpu.VMEM)
    conserved_quantities = pl.pallas_call(
        last_drag_kernel,
        out_shape=shape(8, CX, CY, CZ),
        in_specs=[vmem] * 3,
        out_specs=pl.BlockSpec(memory_space=pl.ANY),
        scratch_shapes=[
            rows_scratch,
            parts_scratch,
            pltpu.VMEM((2, CX, CY, CZ), F32),
            pltpu.SemaphoreType.DMA((4,)),
        ],
        compiler_params=pltpu.CompilerParams(vmem_limit_bytes=VMEM_LIMIT),
        cost_estimate=pl.CostEstimate(flops=0, bytes_accessed=5000000, transcendentals=0),
    )(returned, slots, state)

    ending_thermal_state, ending_electric_voltage = pl.pallas_call(
        thermal_kernel,
        out_shape=[shape(50, 2, CZ), shape(2, CZ)],
        in_specs=[pl.BlockSpec(memory_space=pl.ANY)] + [vmem] * 5,
        scratch_shapes=[pltpu.VMEM((50, 2, CZ), F32), pltpu.SemaphoreType.DMA],
        compiler_params=pltpu.CompilerParams(vmem_limit_bytes=VMEM_LIMIT),
        cost_estimate=pl.CostEstimate(flops=0, bytes_accessed=6600000, transcendentals=0),
    )(
        neutral_thermal_field,
        reciprocal_operators,
        warming_by_height[:, None],
        here_one,
        here_two,
        voltage,
    )
    return (conserved_quantities, ending_thermal_state, ending_electric_voltage)


def solution(mesh):
    in_specs = (
        P("blk", "grp", None),
        P(None, "blk", "grp", None),
        P(None, "blk", "grp", None),
        P("blk", "grp", None),
        P("blk", "grp", None),
        P(("grp", "blk"), None),
        P(("grp", "blk"), None),
        P(("grp", "blk"), None),
        P(None, "blk", None),
        P("blk", None),
        P(),
        P(),
        P(),
    )
    out_specs = (P(None, "blk", "grp", None), P(None, "blk", "grp"), P("blk", "grp"))
    return jax.shard_map(body, mesh=mesh, in_specs=in_specs, out_specs=out_specs, check_vma=False)
```

```python
import functools

import jax
import jax.numpy as jnp
from jax import lax
from jax.experimental import pallas as pl
from jax.experimental.pallas import tpu as pltpu
from jax.sharding import PartitionSpec as P

SWEEPS = 4
HEAT_RATIO = 5.0 / 3.0
TIME_STEP = 0.02
DRAG_RATE = 0.5
CX = 16
CY = 16
CZ = 128
BLOCKS = 32
CAP = 32
SLOTS = BLOCKS * CAP
LATS = 512
BANDS = 8
F32 = jnp.float32
BF16 = jnp.bfloat16
HIGHEST = lax.Precision.HIGHEST
VMEM_LIMIT = 16 * 1024 * 1024


def shape(*dims):
    return jax.ShapeDtypeStruct(dims, F32)


def kernel_call(body, outs, microseconds, scratch=()):
    return pl.pallas_call(
        body,
        out_shape=outs,
        scratch_shapes=list(scratch),
        compiler_params=pltpu.CompilerParams(vmem_limit_bytes=VMEM_LIMIT),
        cost_estimate=pl.CostEstimate(
            flops=0, bytes_accessed=int(microseconds * 3.3e6), transcendentals=0
        ),
    )


def half_slope(before, centre, after, half_limiter):
    forward = after - centre
    backward = centre - before
    low = jnp.minimum(backward, 0.0)
    high = jnp.maximum(backward, 0.0)
    return half_limiter * jnp.minimum(jnp.maximum(forward, low), high)


def root(v):
    return v * lax.rsqrt(jnp.maximum(v, 1e-30))


def side(w, d):
    rho, ux, uy, uz, bx, by, bz, p = w
    u = (ux, uy, uz)
    b = (bx, by, bz)
    e, f = [k for k in range(3) if k != d]
    inverse = 1.0 / rho
    m = [rho * c for c in u]
    across = b[e] * b[e] + b[f] * b[f]
    square = across + b[d] * b[d]
    kinetic = m[0] * ux + m[1] * uy + m[2] * uz
    total = p + 0.5 * square
    energy = 1.5 * p + 0.5 * (kinetic + square)
    along = ux * bx + uy * by + uz * bz
    flux = [None] * 8
    flux[0] = m[d]
    for k in range(3):
        flux[1 + k] = m[k] * u[d] - b[d] * b[k]
        if k != d:
            flux[4 + k] = u[d] * b[k] - b[d] * u[k]
    flux[1 + d] = flux[1 + d] + total
    flux[7] = (energy + total) * u[d] - b[d] * along
    sound = (HEAT_RATIO * p) * inverse
    alfven = square * inverse
    transverse = across * inverse
    gap = sound - alfven
    fast = 0.5 * (sound + alfven + root(gap * gap + 4.0 * sound * transverse))
    speed = jnp.abs(u[d]) + root(fast)
    return flux, [rho, m[0], m[1], m[2], bx, by, bz, energy], speed


def face_flux(left, right, d):
    flux_l, state_l, speed_l = side(left, d)
    flux_r, state_r, speed_r = side(right, d)
    speed = jnp.maximum(speed_l, speed_r)
    out = []
    for k in range(8):
        jump = speed * (state_r[k] - state_l[k])
        if flux_l[k] is None:
            out.append(-jump)
        else:
            out.append(flux_l[k] + flux_r[k] - jump)
    return out


def core():
    return lax.rem(lax.axis_index("blk"), 2)


def substep_kernel(mode, split, refs):
    refs = list(refs)
    w_ref, lim_ref = refs[:2]
    faces = refs[2:6]
    refs = refs[6:]
    if mode == "first":
        lims = [face[16] for face in faces]
    else:
        lims = [refs[0][k] for k in range(4)]
        refs = refs[1:]
    if split:
        uy_ref = refs[0]
        uy_faces = refs[1:5]
        refs = refs[5:]
    if mode == "final":
        out_ref = refs[0]
        outs = ()
        refs = refs[1:]
    else:
        out_ref = refs[0]
        outs = refs[1:5]
        refs = refs[5:]
    if mode == "first":
        for k in range(4):
            refs[0][k] = lims[k]
        refs = refs[1:]
    ext, lim_ext, turned, lim_turned, across, lx, hx = refs
    even = core() == 0
    place_a = jnp.where(even, CX + 2, 0)
    place_b = CX + 2 - place_a

    def halo(which, f, r):
        if split:
            if f == 2:
                return uy_faces[which][r]
            f = f if f < 2 else f - 1
        return faces[which][2 * f + r]

    for f in range(8):
        for r in range(2):
            ext[f, place_a + r] = halo(2, f, r)
            ext[f, place_b + r] = halo(3, f, r)
            turned[f, r] = halo(0, f, r)
            turned[f, CY + 2 + r] = halo(1, f, r)
        centre = uy_ref if split and f == 2 else w_ref.at[f]
        ext[f, 2 : 2 + CX] = centre[...]
        for y in range(CY):
            turned[f, 2 + y] = centre[:, y, :]
    lim_ext[1 : 1 + CX] = 0.5 * lim_ref[...]
    place = jnp.where(even, CX + 1, 0)
    lim_ext[place] = 0.5 * lims[2]
    lim_ext[CX + 1 - place] = 0.5 * lims[3]
    lim_turned[0] = 0.5 * lims[0]
    lim_turned[CY + 1] = 0.5 * lims[1]
    for y in range(CY):
        lim_turned[1 + y] = 0.5 * lim_ref[:, y, :]

    def lowest(w, lim, d):
        left = []
        right = []
        for f in range(8):
            p, q, r, s = w[f, 0], w[f, 1], w[f, 2], w[f, 3]
            left.append(q + half_slope(p, q, r, lim[0]))
            slope = half_slope(q, r, s, lim[1])
            right.append(r - slope)
            lx[d, f] = r + slope
        for f, value in enumerate(face_flux(left, right, d)):
            hx[d, f] = value

    def next_face(w, lim, i, d):
        left = [lx[d, f] for f in range(8)]
        right = []
        for f in range(8):
            after = w[f, i + 3]
            slope = half_slope(w[f, i + 2], after, w[f, i + 4], lim[i + 2])
            right.append(after - slope)
            lx[d, f] = after + slope
        flux = face_flux(left, right, d)
        difference = []
        for f in range(8):
            difference.append(flux[f] - hx[d, f])
            hx[d, f] = flux[f]
        return difference

    lowest(turned, lim_turned, 1)
    lowest(ext, lim_ext, 0)

    def plane(i, carry):
        lim = lim_ext[i + 1]
        w = [ext[f, i + 2] for f in range(8)]
        total = next_face(ext, lim_ext, i, 0)
        for f, value in enumerate(next_face(turned, lim_turned, i, 1)):
            turned[f, i] = value
        left = []
        right = []
        for f in range(8):
            s = half_slope(pltpu.roll(w[f], 1, 1), w[f], pltpu.roll(w[f], CZ - 1, 1), lim)
            left.append(w[f] + s)
            right.append(pltpu.roll(w[f] - s, CZ - 1, 1))
        flux = face_flux(left, right, 2)
        for f in range(8):
            across[f, i] = total[f] + (flux[f] - pltpu.roll(flux[f], 1, 1))
        return carry

    def close(i, carry):
        w = [ext[f, i + 2] for f in range(8)]
        total = [across[f, i] for f in range(8)]
        rho, ux, uy, uz, bx, by, bz, p = w
        m = [rho * ux, rho * uy, rho * uz]
        energy = 1.5 * p + 0.5 * (
            m[0] * ux + m[1] * uy + m[2] * uz + bx * bx + by * by + bz * bz
        )
        state = [rho, m[0], m[1], m[2], bx, by, bz, energy]
        state = [state[f] - (0.5 * TIME_STEP) * total[f] for f in range(8)]
        rho, mx, my, mz, bx, by, bz, energy = state
        if mode == "final":
            result = state
        else:
            inverse = 1.0 / rho
            p = (HEAT_RATIO - 1.0) * (
                energy
                - 0.5 * (mx * mx + my * my + mz * mz) * inverse
                - 0.5 * (bx * bx + by * by + bz * bz)
            )
            result = [rho, mx * inverse, my * inverse, mz * inverse, bx, by, bz, p]
        for f in range(8):
            out_ref[f, i] = result[f]
        return carry

    lax.fori_loop(0, CX, plane, 0, unroll=2)
    for f in range(8):
        for x in range(CX):
            across[f, x] = across[f, x] + turned[f, 0:CY, x, :]
    lax.fori_loop(0, CX, close, 0, unroll=4)
    if mode != "final":
        write_faces(out_ref, outs, mode == "late")


def face_start():
    return jnp.where(core() == 0, CX - 2, 0)


def write_faces(w_ref, outs, late):
    y_low, y_high, x_a, x_b = outs
    start = face_start()
    fields = [f for f in range(8) if not (late and f == 2)]
    for g, f in enumerate(fields):
        for r in range(2):
            y_low[2 * g + r] = w_ref[f, :, r, :]
            y_high[2 * g + r] = w_ref[f, :, CY - 2 + r, :]
            x_a[2 * g + r] = w_ref[f, start + r]
            x_b[2 * g + r] = w_ref[f, CX - 2 - start + r]


def pack_kernel(rho, u, b, p, flags, w_ref, lim_ref, y_low, y_high, x_a, x_b, raw, sems):
    copies = [
        pltpu.make_async_copy(rho, w_ref.at[0], sems.at[0]),
        pltpu.make_async_copy(u, w_ref.at[1:4], sems.at[1]),
        pltpu.make_async_copy(b, w_ref.at[4:7], sems.at[2]),
        pltpu.make_async_copy(p, w_ref.at[7], sems.at[3]),
        pltpu.make_async_copy(flags, raw, sems.at[4]),
    ]
    for copy in copies:
        copy.start()
    for copy in copies:
        copy.wait()
    lim_ref[...] = raw[...].astype(F32)
    write_faces(w_ref, (y_low, y_high, x_a, x_b), False)
    start = jnp.where(core() == 0, CX - 1, 0)
    y_low[16] = lim_ref[:, 0, :]
    y_high[16] = lim_ref[:, CY - 1, :]
    x_a[16] = lim_ref[start]
    x_b[16] = lim_ref[CX - 1 - start]


def substep(mode, split, args):
    scratch = [
        pltpu.VMEM((8, CX + 4, CY, CZ), F32),
        pltpu.VMEM((CX + 2, CY, CZ), F32),
        pltpu.VMEM((8, CY + 4, CX, CZ), F32),
        pltpu.VMEM((CY + 2, CX, CZ), F32),
        pltpu.VMEM((8, CX, CY, CZ), F32),
        pltpu.VMEM((2, 8, CY, CZ), F32),
        pltpu.VMEM((2, 8, CY, CZ), F32),
    ]
    outs = [shape(8, CX, CY, CZ)]
    if mode in ("first", "all"):
        outs += [shape(16, CX, CZ)] * 4
    elif mode == "late":
        outs += [shape(14, CX, CZ)] * 4
    if mode == "first":
        outs += [shape(4, CX, CZ)]

    def body(*refs):
        substep_kernel(mode, split, refs)

    return kernel_call(body, outs, 5.0, scratch)(*args)


def rounded_parts(value, count):
    parts = []
    for _ in range(count):
        part = value.astype(BF16).astype(F32)
        parts.append(part)
        value = value - part
    return parts


def one_hot(positions, extent):
    rows = lax.broadcasted_iota(jnp.int32, (extent, SLOTS), 0)
    return rows == positions.astype(jnp.int32)


def turned_segments(tile):
    tile = jnp.concatenate([tile, tile], axis=0)
    lane = lax.broadcasted_iota(jnp.int32, (8, CZ), 1) // CAP
    row = lax.broadcasted_iota(jnp.int32, (8, CZ), 0)
    same = lane == row % 4
    total = jnp.where(same, tile, 0.0)
    for d in range(1, 4):
        moved = jnp.where(same, pltpu.roll(tile, CAP * d, 1), 0.0)
        total = total + pltpu.roll(moved, 8 - d, 0)
    return total


def spread(rows, out_ref, kept=None):
    half = lax.broadcasted_iota(jnp.int32, (1, CZ), 1) < 2 * CAP
    per = CZ // CAP
    for t in range(SLOTS // CZ):
        tile = turned_segments(rows[0:4, t * CZ : (t + 1) * CZ])
        for j in range(per):
            block = tile[j : j + 1]
            if kept is not None:
                block = jnp.where(half, kept[t * per + j], block)
            out_ref[t * per + j] = block


def collect(block_ref, rows_ref):
    per = CZ // CAP
    for t in range(SLOTS // CZ):
        tile = jnp.concatenate([block_ref[t * per + j] for j in range(per)], axis=0)
        rows_ref[:, t * CZ : (t + 1) * CZ] = turned_segments(tile)


def slot_kernel(owner_ref, rows_ref, out_ref):
    count = owner_ref.shape[0]
    owner = owner_ref[...]
    others = rows_ref[4:5, :].astype(jnp.int32)
    here = lax.broadcasted_iota(jnp.int32, (count, count), 0)
    there = lax.broadcasted_iota(jnp.int32, (count, count), 1)
    earlier = jnp.where((owner == others) & (there < here), 1.0, 0.0)
    rank = jnp.sum(earlier, axis=1, keepdims=True)
    slot = owner * CAP + rank.astype(jnp.int32)
    lanes = lax.broadcasted_iota(jnp.int32, (count, SLOTS), 1)
    table = jnp.where(lanes == slot, 1.0, 0.0).astype(BF16)
    found = jnp.dot(rows_ref[...].astype(BF16), table, preferred_element_type=F32)
    out_ref[...] = found
    out_ref[0:1, :] = found[0:1] + found[5:6] - 1.0
    out_ref[2:3, :] = found[2:3] * CZ + found[3:4]


def payload_kernel(fx, fy, w_ref, y_low, y_high, x_a, x_b, slot_ref, out_ref, fields, rows):
    iota = lax.broadcasted_iota(jnp.int32, (CY, CZ), 0)
    even = core() == 0
    by_low = jnp.where(even, x_b[2 * fy + 1], x_a[2 * fy + 1])
    by_high = jnp.where(even, x_a[2 * fy], x_b[2 * fy])
    bx_low = y_low[2 * fx + 1]
    bx_high = y_high[2 * fx]
    for x in range(CX):
        east = by_high if x == CX - 1 else w_ref[5, x + 1]
        west = by_low if x == 0 else w_ref[5, x - 1]
        bx = w_ref[4, x]
        north = jnp.where(iota == CY - 1, bx_high[x : x + 1, :], pltpu.roll(bx, CY - 1, 0))
        south = jnp.where(iota == 0, bx_low[x : x + 1, :], pltpu.roll(bx, 1, 0))
        p = w_ref[7, x]
        fields[x * CY : (x + 1) * CY, 0:CZ] = 0.5 * (east - west) - 0.5 * (north - south)
        fields[x * CY : (x + 1) * CY, CZ : 2 * CZ] = p * jnp.sqrt(p / w_ref[0, x])
    cells = one_hot(slot_ref[0:1, :], CX * CY).astype(F32).astype(BF16)
    levels = one_hot(slot_ref[1:2, :], CZ)
    across = fields[...].T
    found = jnp.zeros((2 * CZ, SLOTS), F32)
    for part in rounded_parts(across, 3):
        found = found + jnp.dot(part.astype(BF16), cells, preferred_element_type=F32)
    rows[...] = slot_ref[...]
    for v in range(2):
        kept = jnp.where(levels, found[v * CZ : (v + 1) * CZ], 0.0)
        rows[v : v + 1, :] = jnp.sum(kept, axis=0, keepdims=True)
    spread(rows[...], out_ref)


def deposit(rows, column, stack):
    upper = column >= float(LATS)
    place = one_hot(jnp.where(upper, column - LATS, column), LATS).astype(F32).astype(BF16)
    for v in range(2):
        for lon in range(2):
            kept = jnp.where(upper == (lon == 1), rows[v : v + 1, :], 0.0)
            for k, part in enumerate(rounded_parts(kept, 3)):
                at = 4 * k + 2 * v + lon
                stack[at : at + 1, :] = part
    stack[12:16, :] = jnp.zeros((4, SLOTS), F32)
    total = lax.dot_general(
        stack[...].astype(BF16), place, (((1,), (1,)), ((), ())), preferred_element_type=F32
    )
    return total[0:4] + total[4:8] + total[8:12]


def folded(value, out_ref, layer):
    for t in range(LATS // CZ):
        out_ref[layer, 4 * t : 4 * t + 4, :] = value[:, t * CZ : (t + 1) * CZ]


def unfolded(ref, layer):
    return [ref[layer, 4 * t : 4 * t + 4, :] for t in range(LATS // CZ)]


def deposit_first_kernel(block_ref, low_in, high_in, low_out, high_out, sums, column_ref, rows, stack):
    collect(block_ref, rows)
    column_ref[...] = rows[...]
    value = deposit(rows[...], rows[2:3, :], stack)
    count = low_in.shape[0]
    low_out[0:count] = low_in[...]
    high_out[0:count] = high_in[...]
    for out_ref, layer in ((low_out, count), (high_out, count), (sums, 0)):
        folded(value, out_ref, layer)


def scatter(rows, at, slot_ref, parts):
    weight = DRAG_RATE * rows[at + 1 : at + 2, :]
    cells = one_hot(slot_ref[0:1, :], CX * CY).astype(F32).astype(BF16)
    levels = one_hot(slot_ref[1:2, :], CZ)
    for v, value in enumerate((weight * rows[at : at + 1, :], weight)):
        for k, part in enumerate(rounded_parts(value, 2)):
            at = (2 * v + k) * CZ
            parts[at : at + CZ, :] = jnp.where(levels, part, 0.0).astype(BF16)
    total = lax.dot_general(
        cells, parts[...], (((1,), (1,)), ((), ())), preferred_element_type=F32
    )
    first = total[:, 0:CZ] + total[:, CZ : 2 * CZ]
    second = total[:, 2 * CZ : 3 * CZ] + total[:, 3 * CZ :]
    return first.reshape(CX, CY, CZ), second.reshape(CX, CY, CZ)


def drag_kernel(
    block_ref, slot_ref, column_ref, w_ref, out_ref, y_low, y_high, x_a, x_b, sums, rows, parts, stack
):
    collect(block_ref, rows)
    value = deposit(rows[...], column_ref[2:3, :], stack)
    for out_ref_, layer in ((y_low, 2), (y_high, 2), (sums, 0)):
        folded(value, out_ref_, layer)
    first, second = scatter(rows, 2, slot_ref, parts)
    out_ref[...] = w_ref[2] * (1.0 - second) + first
    start = face_start()
    for r in range(2):
        y_low[r] = out_ref[:, r, :]
        y_high[r] = out_ref[:, CY - 2 + r, :]
        x_a[r] = out_ref[start + r]
        x_b[r] = out_ref[CX - 2 - start + r]


def last_drag_kernel(block_ref, slot_ref, u_ref, out_ref, rows, parts, changed, sems):
    kept = [
        pltpu.make_async_copy(u_ref.at[0:2], out_ref.at[0:2], sems.at[0]),
        pltpu.make_async_copy(u_ref.at[3:7], out_ref.at[3:7], sems.at[1]),
    ]
    for copy in kept:
        copy.start()
    collect(block_ref, rows)
    first, second = scatter(rows, 0, slot_ref, parts)
    rho = u_ref[0]
    my = u_ref[2]
    added = rho * first - my * second
    changed[0] = my + added
    changed[1] = u_ref[7] + (my * added + 0.5 * added * added) / rho
    new = [
        pltpu.make_async_copy(changed.at[0], out_ref.at[2], sems.at[2]),
        pltpu.make_async_copy(changed.at[1], out_ref.at[7], sems.at[3]),
    ]
    for copy in new:
        copy.start()
    for copy in kept + new:
        copy.wait()


def base_kernel(inverse_ref, pedersen_ref, warming_ref, thermal_ref, out_ref, factors):
    levels = pedersen_ref.shape[0]
    for band in range(BANDS):
        factors[band : band + 1, :] = jnp.sum(
            pedersen_ref[...] * inverse_ref[band], axis=0, keepdims=True
        )
    once = factors[0:BANDS, :]
    for band in range(BANDS):
        twice = jnp.dot(once, inverse_ref[band], precision=HIGHEST, preferred_element_type=F32)
        factors[BANDS + band : BANDS + band + 1, :] = twice[band : band + 1, :]
    both = factors[...]
    lane_band = lax.broadcasted_iota(jnp.int32, (BANDS, LATS), 1) // (LATS // BANDS)
    own = lane_band == lax.broadcasted_iota(jnp.int32, (BANDS, LATS), 0)

    def pick(values):
        return jnp.sum(jnp.where(own, values, 0.0), axis=0, keepdims=True)

    for lon in range(2):
        field = thermal_ref[:, lon, :]
        found = jnp.dot(both, field, precision=HIGHEST, preferred_element_type=F32)
        out_ref[lon : lon + 1, :] = pick(found[0:BANDS])
        out_ref[2 + lon : 3 + lon, :] = pick(found[BANDS:])
    response = jnp.sum(both * warming_ref[...], axis=1, keepdims=True)
    out_ref[4:5, :] = pick(jnp.broadcast_to(response[0:BANDS], (BANDS, LATS)))
    out_ref[5:6, :] = pick(jnp.broadcast_to(response[BANDS:], (BANDS, LATS)))
    out_ref[6:8, :] = jnp.zeros((2, LATS), F32)


def gather_kernel(
    at, own, low, high, far, potential, base, a_in, b_in, a_out, b_out, here_ref
):
    count = a_in.shape[0]
    a_out[0:count] = a_in[...]
    b_out[0:count] = b_in[...]
    parts = [
        unfolded(own, 0),
        unfolded(low, low.shape[0] - 1),
        unfolded(high, high.shape[0] - 1),
        unfolded(far, 0),
    ]
    for t in range(LATS // CZ):
        lanes = slice(t * CZ, (t + 1) * CZ)
        total = (parts[0][t] + parts[1][t]) + (parts[2][t] + parts[3][t])
        row = (t % 2) * 8
        for out_ref, layer in ((a_out, count), (b_out, count), (here_ref, 0)):
            out_ref[layer + t // 2, row : row + 4, :] = total
            out_ref[layer + t // 2, row + 4 : row + 6, :] = potential[:, lanes]
            out_ref[layer + t // 2, row + 6 : row + 8, :] = base[at : at + 2, lanes]


def flat(ref, first):
    pieces = [ref[first + t // 2, (t % 2) * 8 : (t % 2) * 8 + 8, :] for t in range(LATS // CZ)]
    return jnp.concatenate(pieces, axis=1)


def sweep_kernel(m2, x_a, here_ref, x_b, p2, base, column_ref, *refs):
    payload = refs[0] if len(refs) == 7 else None
    out_v, out_block, out_base, out_here, ext, table = refs[-6:]
    even = core() == 0
    mate = flat(x_a, x_a.shape[0] - 2)
    other = flat(x_b, x_b.shape[0] - 2)
    own = flat(here_ref, 0)
    out_here[...] = own
    around = (
        flat(m2, 0),
        jnp.where(even, other, mate),
        own,
        jnp.where(even, mate, other),
        flat(p2, 0),
    )
    for at, value in enumerate(around):
        for k in range(4):
            ext[k, 2 * at : 2 * at + 2, :] = value[2 * k : 2 * k + 2, :]
    for k in range(4):
        ext[k, 10:16, :] = jnp.ones((6, LATS), F32)
    source = ext[0]
    heat = ext[1]
    potential = ext[2]
    conductance = ext[3] + base[4:5, :] * heat
    lane = lax.broadcasted_iota(jnp.int32, (16, LATS), 1)
    first = lane == 0
    last = lane == LATS - 1

    def up(v):
        return jnp.where(last, 0.0, pltpu.roll(v, LATS - 1, 1))

    def down(v):
        return jnp.where(first, 0.0, pltpu.roll(v, 1, 1))

    east = 0.5 * (conductance + pltpu.roll(conductance, 15, 0))
    west = 0.5 * (conductance + pltpu.roll(conductance, 1, 0))
    north = 0.5 * (conductance + up(conductance))
    south = 0.5 * (conductance + down(conductance))
    inverse = 1.0 / (east + west + north + south)
    for _ in range(SWEEPS):
        potential = (
            east * pltpu.roll(potential, 15, 0)
            + west * pltpu.roll(potential, 1, 0)
            + north * up(potential)
            + south * down(potential)
            - source
        ) * inverse
    ext[2] = potential
    ext[3] = conductance
    out_v[...] = ext[2, 4:6, :]
    out_base[...] = base[...]
    out_base[2:4, :] = base[2:4, :] + base[5:6, :] * own[2:4, :]
    for v in range(2):
        for k, part in enumerate(rounded_parts(ext[2 + v, 4:6, :], 3)):
            table[4 * k + 2 * v : 4 * k + 2 * v + 2, :] = part
    table[12:16, :] = jnp.zeros((4, LATS), F32)
    column = column_ref[2:3, :]
    upper = column >= float(LATS)
    place = one_hot(jnp.where(upper, column - LATS, column), LATS).astype(F32).astype(BF16)
    found = jnp.dot(table[...].astype(BF16), place, preferred_element_type=F32)
    found = found[0:4] + found[4:8] + found[8:12]
    voltage = jnp.where(upper, found[1:2], found[0:1])
    weight = jnp.where(upper, found[3:4], found[2:3])
    sub = lax.broadcasted_iota(jnp.int32, (8, SLOTS), 0)
    rows = jnp.where(sub % 2 == 0, voltage, weight)
    spread(rows, out_block, payload)


def thermal_kernel(
    thermal_ref, inverse_ref, warming_ref, one_ref, two_ref, voltage_ref, out_ref, out_v, own, sem
):
    group = lax.axis_index("grp")
    lanes = pl.ds(pl.multiple_of(group * CZ, CZ), CZ)
    copy = pltpu.make_async_copy(thermal_ref.at[:, :, lanes], own, sem)
    copy.start()
    out_v[...] = voltage_ref[:, lanes]
    copy.wait()
    low_band = lax.broadcasted_iota(jnp.int32, (own.shape[0], CZ), 1) < CZ // 2
    for lon in range(2):
        field = own[:, lon, :]
        for sums in (one_ref, two_ref):
            forced = field + warming_ref[...] * sums[2 + lon : 3 + lon, lanes]
            low, high = (
                jnp.dot(
                    inverse_ref[2 * group + k],
                    forced,
                    precision=HIGHEST,
                    preferred_element_type=F32,
                )
                for k in range(2)
            )
            field = jnp.where(low_band, low, high)
        out_ref[:, lon, :] = field


def shifted(value, axis, by):
    count = lax.axis_size(axis)
    return lax.ppermute(value, axis, [(i, (i + by) % count) for i in range(count)])


def swapped(value, first):
    count = lax.axis_size("blk")
    pairs = [(i, (i + 1) % count) for i in range(first, count, 2)]
    return lax.ppermute(value, "blk", pairs + [(j, i) for i, j in pairs])


def halos(faces):
    y_low, y_high, x_a, x_b = faces
    return (
        shifted(y_high, "grp", 1),
        shifted(y_low, "grp", -1),
        swapped(x_a, 0),
        swapped(x_b, 1),
    )


def halos_and_far(faces, here):
    y_low, y_high, x_a, x_b = faces
    m2, p2 = shifted(here, "blk", 2), shifted(here, "blk", -2)
    m2, p2, x_a = lax.optimization_barrier((m2, p2, x_a))
    return halos((y_low, y_high, x_a, x_b)), m2, p2


def body(
    mass_per_volume,
    flow_vector,
    magnetic_vector,
    thermal_push,
    gradient_clipping_flags,
    tracer_launch_volume,
    tracer_holder_tile,
    holder_local_offset,
    neutral_thermal_field,
    electric_voltage,
    reciprocal_operators,
    warming_by_height,
    pedersen_by_height,
):
    sources = tracer_launch_volume[:, 0]
    columns = holder_local_offset[:, 0]
    zero = jnp.zeros_like(sources)
    line_rows = jnp.stack(
        [
            sources // CZ,
            sources % CZ,
            columns // CZ,
            columns % CZ,
            tracer_holder_tile[:, 0],
            zero + 1,
            zero,
            zero,
        ],
        axis=0,
    ).astype(F32)

    fluid, limiter, *faces = pl.pallas_call(
        pack_kernel,
        out_shape=[pltpu.VMEM((8, CX, CY, CZ), F32), pltpu.VMEM((CX, CY, CZ), F32)]
        + [pltpu.VMEM((17, CX, CZ), F32)] * 4,
        in_specs=[pl.BlockSpec(memory_space=pltpu.HBM)] * 5,
        scratch_shapes=[pltpu.VMEM((CX, CY, CZ), jnp.int32), pltpu.SemaphoreType.DMA((5,))],
        compiler_params=pltpu.CompilerParams(vmem_limit_bytes=56 * 1024 * 1024),
    )(mass_per_volume, flow_vector, magnetic_vector, thermal_push, gradient_clipping_flags)
    first_halos = halos(faces)

    slots = kernel_call(slot_kernel, shape(8, SLOTS), 1.0)(tracer_holder_tile, line_rows)
    base = kernel_call(
        base_kernel, shape(8, LATS), 2.0, [pltpu.VMEM((2 * BANDS, 50), F32)]
    )(
        reciprocal_operators,
        pedersen_by_height[:, None],
        warming_by_height[None, :],
        neutral_thermal_field,
    )

    rows_scratch = pltpu.VMEM((8, SLOTS), F32)
    stack_scratch = pltpu.VMEM((16, SLOTS), F32)
    parts_scratch = pltpu.VMEM((4 * CZ, SLOTS), BF16)

    def payload(w, near, fx, fy):
        return kernel_call(
            functools.partial(payload_kernel, fx, fy),
            shape(BLOCKS, 1, CZ),
            2.0,
            [pltpu.VMEM((CX * CY, 2 * CZ), F32), rows_scratch],
        )(w, *near, slots)

    def exchange(blocks):
        return lax.all_to_all(blocks, "blk", split_axis=0, concat_axis=0, tiled=True)

    def gathered(at, sums, near, far, potential, base_now, x_a, x_b):
        count = x_a.shape[0] + 2
        return kernel_call(
            functools.partial(gather_kernel, at),
            [shape(count, CX, CZ)] * 2 + [shape(2, CX, CZ)],
            0.5,
        )(sums, near[0], near[1], far, potential, base_now, x_a, x_b)

    def swept(m2, x_a, here, x_b, p2, base_now, column, *payload):
        return kernel_call(
            sweep_kernel,
            [shape(2, LATS), shape(BLOCKS, 1, CZ), shape(8, LATS), shape(8, LATS)],
            2.0,
            [pltpu.VMEM((4, 16, LATS), F32), pltpu.VMEM((16, LATS), F32)],
        )(m2, x_a, here, x_b, p2, base_now, column, *payload)

    arrived = exchange(payload(fluid, first_halos, 4, 5))
    fluid, y_low, y_high, x_a, x_b, limits = substep(
        "first", False, (fluid, limiter, *first_halos)
    )
    y_low, y_high, sums, column = kernel_call(
        deposit_first_kernel,
        [shape(17, CX, CZ)] * 2 + [shape(1, CX, CZ), shape(8, SLOTS)],
        1.5,
        [rows_scratch, stack_scratch],
    )(arrived, y_low, y_high)
    near = halos((y_low, y_high, x_a, x_b))
    far = shifted(sums, "grp", 2)
    fluid, y_low, y_high, x_a, x_b = substep(
        "late", False, (fluid, limiter, *near, limits)
    )
    x_a, x_b, here = gathered(0, sums, near, far, electric_voltage, base, x_a, x_b)
    late_halos, m2, p2 = halos_and_far((y_low, y_high, x_a, x_b), here)
    lines = payload(fluid, late_halos, 3, 4)
    voltage, blocks, base_next, here_one = swept(
        m2, late_halos[2], here, late_halos[3], p2, base, column, lines
    )
    arrived = exchange(blocks)
    speed, *faces, sums = kernel_call(
        drag_kernel,
        [shape(CX, CY, CZ)]
        + [shape(3, CX, CZ)] * 2
        + [shape(2, CX, CZ)] * 2
        + [shape(1, CX, CZ)],
        2.0,
        [rows_scratch, parts_scratch, stack_scratch],
    )(arrived, slots, column, fluid)
    speed_halos = halos(faces)
    far = shifted(sums, "grp", 2)
    fluid, y_low, y_high, x_a, x_b = substep(
        "all", True, (fluid, limiter, *late_halos, limits, speed, *speed_halos)
    )
    x_a, x_b, here = gathered(2, sums, speed_halos, far, voltage, base_next, x_a, x_b)
    near, m2, p2 = halos_and_far((y_low, y_high, x_a, x_b), here)
    voltage, blocks, _, here_two = swept(m2, near[2], here, near[3], p2, base_next, column)
    returned = exchange(blocks)
    (state,) = substep("final", False, (fluid, limiter, *near, limits))
    vmem = pl.BlockSpec(memory_space=pltpu.VMEM)
    conserved_quantities = pl.pallas_call(
        last_drag_kernel,
        out_shape=shape(8, CX, CY, CZ),
        in_specs=[vmem] * 3,
        out_specs=pl.BlockSpec(memory_space=pl.ANY),
        scratch_shapes=[
            rows_scratch,
            parts_scratch,
            pltpu.VMEM((2, CX, CY, CZ), F32),
            pltpu.SemaphoreType.DMA((4,)),
        ],
        compiler_params=pltpu.CompilerParams(vmem_limit_bytes=VMEM_LIMIT),
        cost_estimate=pl.CostEstimate(flops=0, bytes_accessed=5000000, transcendentals=0),
    )(returned, slots, state)

    ending_thermal_state, ending_electric_voltage = pl.pallas_call(
        thermal_kernel,
        out_shape=[shape(50, 2, CZ), shape(2, CZ)],
        in_specs=[pl.BlockSpec(memory_space=pl.ANY)] + [vmem] * 5,
        scratch_shapes=[pltpu.VMEM((50, 2, CZ), F32), pltpu.SemaphoreType.DMA],
        compiler_params=pltpu.CompilerParams(vmem_limit_bytes=VMEM_LIMIT),
        cost_estimate=pl.CostEstimate(flops=0, bytes_accessed=6600000, transcendentals=0),
    )(
        neutral_thermal_field,
        reciprocal_operators,
        warming_by_height[:, None],
        here_one,
        here_two,
        voltage,
    )
    return (conserved_quantities, ending_thermal_state, ending_electric_voltage)


def solution(mesh):
    in_specs = (
        P("blk", "grp", None),
        P(None, "blk", "grp", None),
        P(None, "blk", "grp", None),
        P("blk", "grp", None),
        P("blk", "grp", None),
        P(("grp", "blk"), None),
        P(("grp", "blk"), None),
        P(("grp", "blk"), None),
        P(None, "blk", None),
        P("blk", None),
        P(),
        P(),
        P(),
    )
    out_specs = (P(None, "blk", "grp", None), P(None, "blk", "grp"), P("blk", "grp"))
    return jax.shard_map(body, mesh=mesh, in_specs=in_specs, out_specs=out_specs, check_vma=False)
```

```python
import functools

import jax
import jax.numpy as jnp
from jax import lax
from jax.experimental import pallas as pl
from jax.experimental.pallas import tpu as pltpu
from jax.sharding import PartitionSpec as P

SWEEPS = 4
HEAT_RATIO = 5.0 / 3.0
TIME_STEP = 0.02
DRAG_RATE = 0.5
CX = 16
CY = 16
CZ = 128
BLOCKS = 32
CAP = 32
SLOTS = BLOCKS * CAP
LATS = 512
BANDS = 8
F32 = jnp.float32
BF16 = jnp.bfloat16
HIGHEST = lax.Precision.HIGHEST
VMEM_LIMIT = 16 * 1024 * 1024


def shape(*dims):
    return jax.ShapeDtypeStruct(dims, F32)


def kernel_call(body, outs, microseconds, scratch=()):
    return pl.pallas_call(
        body,
        out_shape=outs,
        scratch_shapes=list(scratch),
        compiler_params=pltpu.CompilerParams(vmem_limit_bytes=VMEM_LIMIT),
        cost_estimate=pl.CostEstimate(
            flops=0, bytes_accessed=int(microseconds * 3.3e6), transcendentals=0
        ),
    )


def half_slope(before, centre, after, half_limiter):
    return limited(after - centre, centre - before, half_limiter)


def limited(forward, backward, half_limiter):
    low = jnp.minimum(backward, 0.0)
    high = jnp.maximum(backward, 0.0)
    return half_limiter * jnp.minimum(jnp.maximum(forward, low), high)


def root(v):
    return v * lax.rsqrt(jnp.maximum(v, 1e-30))


def side(w, d):
    rho, ux, uy, uz, bx, by, bz, p = w
    u = (ux, uy, uz)
    b = (bx, by, bz)
    e, f = [k for k in range(3) if k != d]
    inverse = 1.0 / rho
    m = [rho * c for c in u]
    across = b[e] * b[e] + b[f] * b[f]
    square = across + b[d] * b[d]
    kinetic = m[0] * ux + m[1] * uy + m[2] * uz
    total = p + 0.5 * square
    energy = 1.5 * p + 0.5 * (kinetic + square)
    along = ux * bx + uy * by + uz * bz
    flux = [None] * 8
    flux[0] = m[d]
    for k in range(3):
        flux[1 + k] = m[k] * u[d] - b[d] * b[k]
        if k != d:
            flux[4 + k] = u[d] * b[k] - b[d] * u[k]
    flux[1 + d] = flux[1 + d] + total
    flux[7] = (energy + total) * u[d] - b[d] * along
    sound = (HEAT_RATIO * p) * inverse
    alfven = square * inverse
    transverse = across * inverse
    gap = sound - alfven
    fast = 0.5 * (sound + alfven + root(gap * gap + 4.0 * sound * transverse))
    speed = jnp.abs(u[d]) + root(fast)
    return flux, [rho, m[0], m[1], m[2], bx, by, bz, energy], speed


def face_flux(left, right, d):
    flux_l, state_l, speed_l = side(left, d)
    flux_r, state_r, speed_r = side(right, d)
    speed = jnp.maximum(speed_l, speed_r)
    out = []
    for k in range(8):
        jump = speed * (state_r[k] - state_l[k])
        if flux_l[k] is None:
            out.append(-jump)
        else:
            out.append(flux_l[k] + flux_r[k] - jump)
    return out


def core():
    return lax.rem(lax.axis_index("blk"), 2)


def substep_kernel(mode, split, refs):
    refs = list(refs)
    w_ref, lim_ref = refs[:2]
    faces = refs[2:6]
    refs = refs[6:]
    if mode == "first":
        lims = [face[16] for face in faces]
    else:
        lims = [refs[0][k] for k in range(4)]
        refs = refs[1:]
    if split:
        uy_ref = refs[0]
        uy_faces = refs[1:5]
        refs = refs[5:]
    if mode == "final":
        out_ref = refs[0]
        outs = ()
        refs = refs[1:]
    else:
        out_ref = refs[0]
        outs = refs[1:5]
        refs = refs[5:]
    if mode == "first":
        for k in range(4):
            refs[0][k] = lims[k]
        refs = refs[1:]
    ext, lim_ext, turned, lim_turned, across, lx, hx, fx = refs
    even = core() == 0
    place_a = jnp.where(even, CX + 2, 0)
    place_b = CX + 2 - place_a

    def halo(which, f, r):
        if split:
            if f == 2:
                return uy_faces[which][r]
            f = f if f < 2 else f - 1
        return faces[which][2 * f + r]

    for f in range(8):
        for r in range(2):
            ext[f, place_a + r] = halo(2, f, r)
            ext[f, place_b + r] = halo(3, f, r)
            turned[f, r] = halo(0, f, r)
            turned[f, CY + 2 + r] = halo(1, f, r)
        centre = uy_ref if split and f == 2 else w_ref.at[f]
        ext[f, 2 : 2 + CX] = centre[...]
        for y in range(CY):
            turned[f, 2 + y] = centre[:, y, :]
    lim_ext[1 : 1 + CX] = 0.5 * lim_ref[...]
    place = jnp.where(even, CX + 1, 0)
    lim_ext[place] = 0.5 * lims[2]
    lim_ext[CX + 1 - place] = 0.5 * lims[3]
    lim_turned[0] = 0.5 * lims[0]
    lim_turned[CY + 1] = 0.5 * lims[1]
    for y in range(CY):
        lim_turned[1 + y] = 0.5 * lim_ref[:, y, :]

    def lowest(w, lim, d):
        left = []
        right = []
        for f in range(8):
            p, q, r, s = w[f, 0], w[f, 1], w[f, 2], w[f, 3]
            left.append(q + half_slope(p, q, r, lim[0]))
            slope = half_slope(q, r, s, lim[1])
            right.append(r - slope)
            lx[d, f] = r + slope
            fx[d, f] = s - r
        for f, value in enumerate(face_flux(left, right, d)):
            hx[d, f] = value

    def next_face(w, lim, i, d):
        left = [lx[d, f] for f in range(8)]
        right = []
        for f in range(8):
            after = w[f, i + 3]
            forward = w[f, i + 4] - after
            slope = limited(forward, fx[d, f], lim[i + 2])
            fx[d, f] = forward
            right.append(after - slope)
            lx[d, f] = after + slope
        flux = face_flux(left, right, d)
        difference = []
        for f in range(8):
            difference.append(flux[f] - hx[d, f])
            hx[d, f] = flux[f]
        return difference

    lowest(turned, lim_turned, 1)
    lowest(ext, lim_ext, 0)

    def plane(i, carry):
        lim = lim_ext[i + 1]
        w = [ext[f, i + 2] for f in range(8)]
        total = next_face(ext, lim_ext, i, 0)
        for f, value in enumerate(next_face(turned, lim_turned, i, 1)):
            turned[f, i] = value
        left = []
        right = []
        for f in range(8):
            s = half_slope(pltpu.roll(w[f], 1, 1), w[f], pltpu.roll(w[f], CZ - 1, 1), lim)
            left.append(w[f] + s)
            right.append(pltpu.roll(w[f] - s, CZ - 1, 1))
        flux = face_flux(left, right, 2)
        for f in range(8):
            across[f, i] = total[f] + (flux[f] - pltpu.roll(flux[f], 1, 1))
        return carry

    def close(i, carry):
        w = [ext[f, i + 2] for f in range(8)]
        total = [across[f, i] for f in range(8)]
        rho, ux, uy, uz, bx, by, bz, p = w
        m = [rho * ux, rho * uy, rho * uz]
        energy = 1.5 * p + 0.5 * (
            m[0] * ux + m[1] * uy + m[2] * uz + bx * bx + by * by + bz * bz
        )
        state = [rho, m[0], m[1], m[2], bx, by, bz, energy]
        state = [state[f] - (0.5 * TIME_STEP) * total[f] for f in range(8)]
        rho, mx, my, mz, bx, by, bz, energy = state
        if mode == "final":
            result = state
        else:
            inverse = 1.0 / rho
            p = (HEAT_RATIO - 1.0) * (
                energy
                - 0.5 * (mx * mx + my * my + mz * mz) * inverse
                - 0.5 * (bx * bx + by * by + bz * bz)
            )
            result = [rho, mx * inverse, my * inverse, mz * inverse, bx, by, bz, p]
        for f in range(8):
            out_ref[f, i] = result[f]
        return carry

    lax.fori_loop(0, CX, plane, 0, unroll=2)
    for f in range(8):
        for x in range(CX):
            across[f, x] = across[f, x] + turned[f, 0:CY, x, :]
    lax.fori_loop(0, CX, close, 0, unroll=4)
    if mode != "final":
        write_faces(out_ref, outs, mode == "late")


def face_start():
    return jnp.where(core() == 0, CX - 2, 0)


def write_faces(w_ref, outs, late):
    y_low, y_high, x_a, x_b = outs
    start = face_start()
    fields = [f for f in range(8) if not (late and f == 2)]
    for g, f in enumerate(fields):
        for r in range(2):
            y_low[2 * g + r] = w_ref[f, :, r, :]
            y_high[2 * g + r] = w_ref[f, :, CY - 2 + r, :]
            x_a[2 * g + r] = w_ref[f, start + r]
            x_b[2 * g + r] = w_ref[f, CX - 2 - start + r]


def pack_kernel(rho, u, b, p, flags, w_ref, lim_ref, y_low, y_high, x_a, x_b, raw, sems):
    copies = [
        pltpu.make_async_copy(rho, w_ref.at[0], sems.at[0]),
        pltpu.make_async_copy(u, w_ref.at[1:4], sems.at[1]),
        pltpu.make_async_copy(b, w_ref.at[4:7], sems.at[2]),
        pltpu.make_async_copy(p, w_ref.at[7], sems.at[3]),
        pltpu.make_async_copy(flags, raw, sems.at[4]),
    ]
    for copy in copies:
        copy.start()
    for copy in copies:
        copy.wait()
    lim_ref[...] = raw[...].astype(F32)
    write_faces(w_ref, (y_low, y_high, x_a, x_b), False)
    start = jnp.where(core() == 0, CX - 1, 0)
    y_low[16] = lim_ref[:, 0, :]
    y_high[16] = lim_ref[:, CY - 1, :]
    x_a[16] = lim_ref[start]
    x_b[16] = lim_ref[CX - 1 - start]


def substep(mode, split, args):
    scratch = [
        pltpu.VMEM((8, CX + 4, CY, CZ), F32),
        pltpu.VMEM((CX + 2, CY, CZ), F32),
        pltpu.VMEM((8, CY + 4, CX, CZ), F32),
        pltpu.VMEM((CY + 2, CX, CZ), F32),
        pltpu.VMEM((8, CX, CY, CZ), F32),
        pltpu.VMEM((2, 8, CY, CZ), F32),
        pltpu.VMEM((2, 8, CY, CZ), F32),
        pltpu.VMEM((2, 8, CY, CZ), F32),
    ]
    outs = [shape(8, CX, CY, CZ)]
    if mode in ("first", "all"):
        outs += [shape(16, CX, CZ)] * 4
    elif mode == "late":
        outs += [shape(14, CX, CZ)] * 4
    if mode == "first":
        outs += [shape(4, CX, CZ)]

    def body(*refs):
        substep_kernel(mode, split, refs)

    return kernel_call(body, outs, 5.0, scratch)(*args)


def rounded_parts(value, count):
    parts = []
    for _ in range(count):
        part = value.astype(BF16).astype(F32)
        parts.append(part)
        value = value - part
    return parts


def one_hot(positions, extent):
    rows = lax.broadcasted_iota(jnp.int32, (extent, SLOTS), 0)
    return rows == positions.astype(jnp.int32)


def turned_segments(tile):
    tile = jnp.concatenate([tile, tile], axis=0)
    lane = lax.broadcasted_iota(jnp.int32, (8, CZ), 1) // CAP
    row = lax.broadcasted_iota(jnp.int32, (8, CZ), 0)
    same = lane == row % 4
    total = jnp.where(same, tile, 0.0)
    for d in range(1, 4):
        moved = jnp.where(same, pltpu.roll(tile, CAP * d, 1), 0.0)
        total = total + pltpu.roll(moved, 8 - d, 0)
    return total


def spread(rows, out_ref, kept=None):
    half = lax.broadcasted_iota(jnp.int32, (1, CZ), 1) < 2 * CAP
    per = CZ // CAP
    for t in range(SLOTS // CZ):
        tile = turned_segments(rows[0:4, t * CZ : (t + 1) * CZ])
        for j in range(per):
            block = tile[j : j + 1]
            if kept is not None:
                block = jnp.where(half, kept[t * per + j], block)
            out_ref[t * per + j] = block


def collect(block_ref, rows_ref):
    per = CZ // CAP
    for t in range(SLOTS // CZ):
        tile = jnp.concatenate([block_ref[t * per + j] for j in range(per)], axis=0)
        rows_ref[:, t * CZ : (t + 1) * CZ] = turned_segments(tile)


def slot_kernel(owner_ref, rows_ref, out_ref):
    count = owner_ref.shape[0]
    owner = owner_ref[...]
    others = rows_ref[4:5, :].astype(jnp.int32)
    here = lax.broadcasted_iota(jnp.int32, (count, count), 0)
    there = lax.broadcasted_iota(jnp.int32, (count, count), 1)
    earlier = jnp.where((owner == others) & (there < here), 1.0, 0.0)
    rank = jnp.sum(earlier, axis=1, keepdims=True)
    slot = owner * CAP + rank.astype(jnp.int32)
    lanes = lax.broadcasted_iota(jnp.int32, (count, SLOTS), 1)
    table = jnp.where(lanes == slot, 1.0, 0.0).astype(BF16)
    found = jnp.dot(rows_ref[...].astype(BF16), table, preferred_element_type=F32)
    out_ref[...] = found
    out_ref[0:1, :] = found[0:1] + found[5:6] - 1.0
    out_ref[2:3, :] = found[2:3] * CZ + found[3:4]


def payload_kernel(fx, fy, w_ref, y_low, y_high, x_a, x_b, slot_ref, out_ref, fields, rows):
    iota = lax.broadcasted_iota(jnp.int32, (CY, CZ), 0)
    even = core() == 0
    by_low = jnp.where(even, x_b[2 * fy + 1], x_a[2 * fy + 1])
    by_high = jnp.where(even, x_a[2 * fy], x_b[2 * fy])
    bx_low = y_low[2 * fx + 1]
    bx_high = y_high[2 * fx]
    for x in range(CX):
        east = by_high if x == CX - 1 else w_ref[5, x + 1]
        west = by_low if x == 0 else w_ref[5, x - 1]
        bx = w_ref[4, x]
        north = jnp.where(iota == CY - 1, bx_high[x : x + 1, :], pltpu.roll(bx, CY - 1, 0))
        south = jnp.where(iota == 0, bx_low[x : x + 1, :], pltpu.roll(bx, 1, 0))
        p = w_ref[7, x]
        fields[x * CY : (x + 1) * CY, 0:CZ] = 0.5 * (east - west) - 0.5 * (north - south)
        fields[x * CY : (x + 1) * CY, CZ : 2 * CZ] = p * jnp.sqrt(p / w_ref[0, x])
    cells = one_hot(slot_ref[0:1, :], CX * CY).astype(F32).astype(BF16)
    levels = one_hot(slot_ref[1:2, :], CZ)
    across = fields[...].T
    found = jnp.zeros((2 * CZ, SLOTS), F32)
    for part in rounded_parts(across, 3):
        found = found + jnp.dot(part.astype(BF16), cells, preferred_element_type=F32)
    rows[...] = slot_ref[...]
    for v in range(2):
        kept = jnp.where(levels, found[v * CZ : (v + 1) * CZ], 0.0)
        rows[v : v + 1, :] = jnp.sum(kept, axis=0, keepdims=True)
    spread(rows[...], out_ref)


def deposit(rows, column, stack):
    upper = column >= float(LATS)
    place = one_hot(jnp.where(upper, column - LATS, column), LATS).astype(F32).astype(BF16)
    for v in range(2):
        for lon in range(2):
            kept = jnp.where(upper == (lon == 1), rows[v : v + 1, :], 0.0)
            for k, part in enumerate(rounded_parts(kept, 3)):
                at = 4 * k + 2 * v + lon
                stack[at : at + 1, :] = part
    stack[12:16, :] = jnp.zeros((4, SLOTS), F32)
    total = lax.dot_general(
        stack[...].astype(BF16), place, (((1,), (1,)), ((), ())), preferred_element_type=F32
    )
    return total[0:4] + total[4:8] + total[8:12]


def folded(value, out_ref, layer):
    for t in range(LATS // CZ):
        out_ref[layer, 4 * t : 4 * t + 4, :] = value[:, t * CZ : (t + 1) * CZ]


def unfolded(ref, layer):
    return [ref[layer, 4 * t : 4 * t + 4, :] for t in range(LATS // CZ)]


def deposit_first_kernel(block_ref, low_in, high_in, low_out, high_out, sums, column_ref, rows, stack):
    collect(block_ref, rows)
    column_ref[...] = rows[...]
    value = deposit(rows[...], rows[2:3, :], stack)
    count = low_in.shape[0]
    low_out[0:count] = low_in[...]
    high_out[0:count] = high_in[...]
    for out_ref, layer in ((low_out, count), (high_out, count), (sums, 0)):
        folded(value, out_ref, layer)


def scatter(rows, at, slot_ref, parts):
    weight = DRAG_RATE * rows[at + 1 : at + 2, :]
    cells = one_hot(slot_ref[0:1, :], CX * CY).astype(F32).astype(BF16)
    levels = one_hot(slot_ref[1:2, :], CZ)
    for v, value in enumerate((weight * rows[at : at + 1, :], weight)):
        for k, part in enumerate(rounded_parts(value, 2)):
            at = (2 * v + k) * CZ
            parts[at : at + CZ, :] = jnp.where(levels, part, 0.0).astype(BF16)
    total = lax.dot_general(
        cells, parts[...], (((1,), (1,)), ((), ())), preferred_element_type=F32
    )
    first = total[:, 0:CZ] + total[:, CZ : 2 * CZ]
    second = total[:, 2 * CZ : 3 * CZ] + total[:, 3 * CZ :]
    return first.reshape(CX, CY, CZ), second.reshape(CX, CY, CZ)


def drag_kernel(
    block_ref, slot_ref, column_ref, w_ref, out_ref, y_low, y_high, x_a, x_b, sums, rows, parts, stack
):
    collect(block_ref, rows)
    value = deposit(rows[...], column_ref[2:3, :], stack)
    for out_ref_, layer in ((y_low, 2), (y_high, 2), (sums, 0)):
        folded(value, out_ref_, layer)
    first, second = scatter(rows, 2, slot_ref, parts)
    out_ref[...] = w_ref[2] * (1.0 - second) + first
    start = face_start()
    for r in range(2):
        y_low[r] = out_ref[:, r, :]
        y_high[r] = out_ref[:, CY - 2 + r, :]
        x_a[r] = out_ref[start + r]
        x_b[r] = out_ref[CX - 2 - start + r]


def last_drag_kernel(block_ref, slot_ref, u_ref, out_ref, rows, parts, changed, sems):
    kept = [
        pltpu.make_async_copy(u_ref.at[0:2], out_ref.at[0:2], sems.at[0]),
        pltpu.make_async_copy(u_ref.at[3:7], out_ref.at[3:7], sems.at[1]),
    ]
    for copy in kept:
        copy.start()
    collect(block_ref, rows)
    first, second = scatter(rows, 0, slot_ref, parts)
    rho = u_ref[0]
    my = u_ref[2]
    added = rho * first - my * second
    changed[0] = my + added
    changed[1] = u_ref[7] + (my * added + 0.5 * added * added) / rho
    new = [
        pltpu.make_async_copy(changed.at[0], out_ref.at[2], sems.at[2]),
        pltpu.make_async_copy(changed.at[1], out_ref.at[7], sems.at[3]),
    ]
    for copy in new:
        copy.start()
    for copy in kept + new:
        copy.wait()


def base_kernel(inverse_ref, pedersen_ref, warming_ref, thermal_ref, out_ref, factors):
    levels = pedersen_ref.shape[0]
    for band in range(BANDS):
        factors[band : band + 1, :] = jnp.sum(
            pedersen_ref[...] * inverse_ref[band], axis=0, keepdims=True
        )
    once = factors[0:BANDS, :]
    for band in range(BANDS):
        twice = jnp.dot(once, inverse_ref[band], precision=HIGHEST, preferred_element_type=F32)
        factors[BANDS + band : BANDS + band + 1, :] = twice[band : band + 1, :]
    both = factors[...]
    lane_band = lax.broadcasted_iota(jnp.int32, (BANDS, LATS), 1) // (LATS // BANDS)
    own = lane_band == lax.broadcasted_iota(jnp.int32, (BANDS, LATS), 0)

    def pick(values):
        return jnp.sum(jnp.where(own, values, 0.0), axis=0, keepdims=True)

    for lon in range(2):
        field = thermal_ref[:, lon, :]
        found = jnp.dot(both, field, precision=HIGHEST, preferred_element_type=F32)
        out_ref[lon : lon + 1, :] = pick(found[0:BANDS])
        out_ref[2 + lon : 3 + lon, :] = pick(found[BANDS:])
    response = jnp.sum(both * warming_ref[...], axis=1, keepdims=True)
    out_ref[4:5, :] = pick(jnp.broadcast_to(response[0:BANDS], (BANDS, LATS)))
    out_ref[5:6, :] = pick(jnp.broadcast_to(response[BANDS:], (BANDS, LATS)))
    out_ref[6:8, :] = jnp.zeros((2, LATS), F32)


def gather_kernel(
    at, own, low, high, far, potential, base, a_in, b_in, a_out, b_out, here_ref
):
    count = a_in.shape[0]
    a_out[0:count] = a_in[...]
    b_out[0:count] = b_in[...]
    parts = [
        unfolded(own, 0),
        unfolded(low, low.shape[0] - 1),
        unfolded(high, high.shape[0] - 1),
        unfolded(far, 0),
    ]
    for t in range(LATS // CZ):
        lanes = slice(t * CZ, (t + 1) * CZ)
        total = (parts[0][t] + parts[1][t]) + (parts[2][t] + parts[3][t])
        row = (t % 2) * 8
        for out_ref, layer in ((a_out, count), (b_out, count), (here_ref, 0)):
            out_ref[layer + t // 2, row : row + 4, :] = total
            out_ref[layer + t // 2, row + 4 : row + 6, :] = potential[:, lanes]
            out_ref[layer + t // 2, row + 6 : row + 8, :] = base[at : at + 2, lanes]


def flat(ref, first):
    pieces = [ref[first + t // 2, (t % 2) * 8 : (t % 2) * 8 + 8, :] for t in range(LATS // CZ)]
    return jnp.concatenate(pieces, axis=1)


def sweep_kernel(m2, x_a, here_ref, x_b, p2, base, column_ref, *refs):
    payload = refs[0] if len(refs) == 7 else None
    out_v, out_block, out_base, out_here, ext, table = refs[-6:]
    even = core() == 0
    mate = flat(x_a, x_a.shape[0] - 2)
    other = flat(x_b, x_b.shape[0] - 2)
    own = flat(here_ref, 0)
    out_here[...] = own
    around = (
        flat(m2, 0),
        jnp.where(even, other, mate),
        own,
        jnp.where(even, mate, other),
        flat(p2, 0),
    )
    for at, value in enumerate(around):
        for k in range(4):
            ext[k, 2 * at : 2 * at + 2, :] = value[2 * k : 2 * k + 2, :]
    for k in range(4):
        ext[k, 10:16, :] = jnp.ones((6, LATS), F32)
    source = ext[0]
    heat = ext[1]
    potential = ext[2]
    conductance = ext[3] + base[4:5, :] * heat
    lane = lax.broadcasted_iota(jnp.int32, (16, LATS), 1)
    first = lane == 0
    last = lane == LATS - 1

    def up(v):
        return jnp.where(last, 0.0, pltpu.roll(v, LATS - 1, 1))

    def down(v):
        return jnp.where(first, 0.0, pltpu.roll(v, 1, 1))

    east = 0.5 * (conductance + pltpu.roll(conductance, 15, 0))
    west = 0.5 * (conductance + pltpu.roll(conductance, 1, 0))
    north = 0.5 * (conductance + up(conductance))
    south = 0.5 * (conductance + down(conductance))
    inverse = 1.0 / (east + west + north + south)
    for _ in range(SWEEPS):
        potential = (
            east * pltpu.roll(potential, 15, 0)
            + west * pltpu.roll(potential, 1, 0)
            + north * up(potential)
            + south * down(potential)
            - source
        ) * inverse
    ext[2] = potential
    ext[3] = conductance
    out_v[...] = ext[2, 4:6, :]
    out_base[...] = base[...]
    out_base[2:4, :] = base[2:4, :] + base[5:6, :] * own[2:4, :]
    for v in range(2):
        for k, part in enumerate(rounded_parts(ext[2 + v, 4:6, :], 3)):
            table[4 * k + 2 * v : 4 * k + 2 * v + 2, :] = part
    table[12:16, :] = jnp.zeros((4, LATS), F32)
    column = column_ref[2:3, :]
    upper = column >= float(LATS)
    place = one_hot(jnp.where(upper, column - LATS, column), LATS).astype(F32).astype(BF16)
    found = jnp.dot(table[...].astype(BF16), place, preferred_element_type=F32)
    found = found[0:4] + found[4:8] + found[8:12]
    voltage = jnp.where(upper, found[1:2], found[0:1])
    weight = jnp.where(upper, found[3:4], found[2:3])
    sub = lax.broadcasted_iota(jnp.int32, (8, SLOTS), 0)
    rows = jnp.where(sub % 2 == 0, voltage, weight)
    spread(rows, out_block, payload)


def thermal_kernel(
    thermal_ref, inverse_ref, warming_ref, one_ref, two_ref, voltage_ref, out_ref, out_v, own, sem
):
    group = lax.axis_index("grp")
    lanes = pl.ds(pl.multiple_of(group * CZ, CZ), CZ)
    copy = pltpu.make_async_copy(thermal_ref.at[:, :, lanes], own, sem)
    copy.start()
    out_v[...] = voltage_ref[:, lanes]
    copy.wait()
    low_band = lax.broadcasted_iota(jnp.int32, (own.shape[0], CZ), 1) < CZ // 2
    for lon in range(2):
        field = own[:, lon, :]
        for sums in (one_ref, two_ref):
            forced = field + warming_ref[...] * sums[2 + lon : 3 + lon, lanes]
            low, high = (
                jnp.dot(
                    inverse_ref[2 * group + k],
                    forced,
                    precision=HIGHEST,
                    preferred_element_type=F32,
                )
                for k in range(2)
            )
            field = jnp.where(low_band, low, high)
        out_ref[:, lon, :] = field


def shifted(value, axis, by):
    count = lax.axis_size(axis)
    return lax.ppermute(value, axis, [(i, (i + by) % count) for i in range(count)])


def swapped(value, first):
    count = lax.axis_size("blk")
    pairs = [(i, (i + 1) % count) for i in range(first, count, 2)]
    return lax.ppermute(value, "blk", pairs + [(j, i) for i, j in pairs])


def halos(faces):
    y_low, y_high, x_a, x_b = faces
    return (
        shifted(y_high, "grp", 1),
        shifted(y_low, "grp", -1),
        swapped(x_a, 0),
        swapped(x_b, 1),
    )


def halos_and_far(faces, here):
    y_low, y_high, x_a, x_b = faces
    m2, p2 = shifted(here, "blk", 2), shifted(here, "blk", -2)
    m2, p2, x_a = lax.optimization_barrier((m2, p2, x_a))
    return halos((y_low, y_high, x_a, x_b)), m2, p2


def body(
    mass_per_volume,
    flow_vector,
    magnetic_vector,
    thermal_push,
    gradient_clipping_flags,
    tracer_launch_volume,
    tracer_holder_tile,
    holder_local_offset,
    neutral_thermal_field,
    electric_voltage,
    reciprocal_operators,
    warming_by_height,
    pedersen_by_height,
):
    sources = tracer_launch_volume[:, 0]
    columns = holder_local_offset[:, 0]
    zero = jnp.zeros_like(sources)
    line_rows = jnp.stack(
        [
            sources // CZ,
            sources % CZ,
            columns // CZ,
            columns % CZ,
            tracer_holder_tile[:, 0],
            zero + 1,
            zero,
            zero,
        ],
        axis=0,
    ).astype(F32)

    fluid, limiter, *faces = pl.pallas_call(
        pack_kernel,
        out_shape=[pltpu.VMEM((8, CX, CY, CZ), F32), pltpu.VMEM((CX, CY, CZ), F32)]
        + [pltpu.VMEM((17, CX, CZ), F32)] * 4,
        in_specs=[pl.BlockSpec(memory_space=pltpu.HBM)] * 5,
        scratch_shapes=[pltpu.VMEM((CX, CY, CZ), jnp.int32), pltpu.SemaphoreType.DMA((5,))],
        compiler_params=pltpu.CompilerParams(vmem_limit_bytes=56 * 1024 * 1024),
    )(mass_per_volume, flow_vector, magnetic_vector, thermal_push, gradient_clipping_flags)
    first_halos = halos(faces)

    slots = kernel_call(slot_kernel, shape(8, SLOTS), 1.0)(tracer_holder_tile, line_rows)
    base = kernel_call(
        base_kernel, shape(8, LATS), 2.0, [pltpu.VMEM((2 * BANDS, 50), F32)]
    )(
        reciprocal_operators,
        pedersen_by_height[:, None],
        warming_by_height[None, :],
        neutral_thermal_field,
    )

    rows_scratch = pltpu.VMEM((8, SLOTS), F32)
    stack_scratch = pltpu.VMEM((16, SLOTS), F32)
    parts_scratch = pltpu.VMEM((4 * CZ, SLOTS), BF16)

    def payload(w, near, fx, fy):
        return kernel_call(
            functools.partial(payload_kernel, fx, fy),
            shape(BLOCKS, 1, CZ),
            2.0,
            [pltpu.VMEM((CX * CY, 2 * CZ), F32), rows_scratch],
        )(w, *near, slots)

    def exchange(blocks):
        return lax.all_to_all(blocks, "blk", split_axis=0, concat_axis=0, tiled=True)

    def gathered(at, sums, near, far, potential, base_now, x_a, x_b):
        count = x_a.shape[0] + 2
        return kernel_call(
            functools.partial(gather_kernel, at),
            [shape(count, CX, CZ)] * 2 + [shape(2, CX, CZ)],
            0.5,
        )(sums, near[0], near[1], far, potential, base_now, x_a, x_b)

    def swept(m2, x_a, here, x_b, p2, base_now, column, *payload):
        return kernel_call(
            sweep_kernel,
            [shape(2, LATS), shape(BLOCKS, 1, CZ), shape(8, LATS), shape(8, LATS)],
            2.0,
            [pltpu.VMEM((4, 16, LATS), F32), pltpu.VMEM((16, LATS), F32)],
        )(m2, x_a, here, x_b, p2, base_now, column, *payload)

    arrived = exchange(payload(fluid, first_halos, 4, 5))
    fluid, y_low, y_high, x_a, x_b, limits = substep(
        "first", False, (fluid, limiter, *first_halos)
    )
    y_low, y_high, sums, column = kernel_call(
        deposit_first_kernel,
        [shape(17, CX, CZ)] * 2 + [shape(1, CX, CZ), shape(8, SLOTS)],
        1.5,
        [rows_scratch, stack_scratch],
    )(arrived, y_low, y_high)
    near = halos((y_low, y_high, x_a, x_b))
    far = shifted(sums, "grp", 2)
    fluid, y_low, y_high, x_a, x_b = substep(
        "late", False, (fluid, limiter, *near, limits)
    )
    x_a, x_b, here = gathered(0, sums, near, far, electric_voltage, base, x_a, x_b)
    late_halos, m2, p2 = halos_and_far((y_low, y_high, x_a, x_b), here)
    lines = payload(fluid, late_halos, 3, 4)
    voltage, blocks, base_next, here_one = swept(
        m2, late_halos[2], here, late_halos[3], p2, base, column, lines
    )
    arrived = exchange(blocks)
    speed, *faces, sums = kernel_call(
        drag_kernel,
        [shape(CX, CY, CZ)]
        + [shape(3, CX, CZ)] * 2
        + [shape(2, CX, CZ)] * 2
        + [shape(1, CX, CZ)],
        2.0,
        [rows_scratch, parts_scratch, stack_scratch],
    )(arrived, slots, column, fluid)
    speed_halos = halos(faces)
    far = shifted(sums, "grp", 2)
    fluid, y_low, y_high, x_a, x_b = substep(
        "all", True, (fluid, limiter, *late_halos, limits, speed, *speed_halos)
    )
    x_a, x_b, here = gathered(2, sums, speed_halos, far, voltage, base_next, x_a, x_b)
    near, m2, p2 = halos_and_far((y_low, y_high, x_a, x_b), here)
    voltage, blocks, _, here_two = swept(m2, near[2], here, near[3], p2, base_next, column)
    returned = exchange(blocks)
    (state,) = substep("final", False, (fluid, limiter, *near, limits))
    vmem = pl.BlockSpec(memory_space=pltpu.VMEM)
    conserved_quantities = pl.pallas_call(
        last_drag_kernel,
        out_shape=shape(8, CX, CY, CZ),
        in_specs=[vmem] * 3,
        out_specs=pl.BlockSpec(memory_space=pl.ANY),
        scratch_shapes=[
            rows_scratch,
            parts_scratch,
            pltpu.VMEM((2, CX, CY, CZ), F32),
            pltpu.SemaphoreType.DMA((4,)),
        ],
        compiler_params=pltpu.CompilerParams(vmem_limit_bytes=VMEM_LIMIT),
        cost_estimate=pl.CostEstimate(flops=0, bytes_accessed=5000000, transcendentals=0),
    )(returned, slots, state)

    ending_thermal_state, ending_electric_voltage = pl.pallas_call(
        thermal_kernel,
        out_shape=[shape(50, 2, CZ), shape(2, CZ)],
        in_specs=[pl.BlockSpec(memory_space=pl.ANY)] + [vmem] * 5,
        scratch_shapes=[pltpu.VMEM((50, 2, CZ), F32), pltpu.SemaphoreType.DMA],
        compiler_params=pltpu.CompilerParams(vmem_limit_bytes=VMEM_LIMIT),
        cost_estimate=pl.CostEstimate(flops=0, bytes_accessed=6600000, transcendentals=0),
    )(
        neutral_thermal_field,
        reciprocal_operators,
        warming_by_height[:, None],
        here_one,
        here_two,
        voltage,
    )
    return (conserved_quantities, ending_thermal_state, ending_electric_voltage)


def solution(mesh):
    in_specs = (
        P("blk", "grp", None),
        P(None, "blk", "grp", None),
        P(None, "blk", "grp", None),
        P("blk", "grp", None),
        P("blk", "grp", None),
        P(("grp", "blk"), None),
        P(("grp", "blk"), None),
        P(("grp", "blk"), None),
        P(None, "blk", None),
        P("blk", None),
        P(),
        P(),
        P(),
    )
    out_specs = (P(None, "blk", "grp", None), P(None, "blk", "grp"), P("blk", "grp"))
    return jax.shard_map(body, mesh=mesh, in_specs=in_specs, out_specs=out_specs, check_vma=False)
```
